32 devices in a mesh: slab: 8 (over z, x), pencil: 4 (over y, core).
Axes of the slice: x: 2, y: 2, z: 4, core: 2. Of those that a mesh axis runs over, the one named last changes fastest.
Arguments:
- basis: bfloat16 [88, 64, 128, 128], P(None, 'slab', 'pencil'), may hold values from -6 to 6
- image: bfloat16 [88, 64, 128, 128], P(None, 'slab', 'pencil'), may hold values from -6.3 to 6.3
- material: int32 [64, 128, 128], P('slab', 'pencil'), may hold values from 0 to 3
- picked: int32 [32], replicated, may hold values from 0 to 87, as said below
Outputs:
- recycle_out: float32 [32, 64, 128, 128], P(None, 'slab', 'pencil')
- images_out: float32 [32, 64, 128, 128], P(None, 'slab', 'pencil')
The draws below stay inside these ranges and needn't reach their ends.
Inputs may be any that keep to these rules, and one draw needn't show every extreme that they name: `picked`: 32 distinct column numbers.
All inputs are finite; a program needn't handle non-finite values.
Results may differ from the reference program's by a relative error of at most 0.0061.
Values may be sent and summed in bfloat16 or wider, within the bound.
A program may use at most 128 MiB of HBM per device.

```python
import jax
import jax.numpy as jnp
from jax import lax

RECYCLE = 32
COLS = 88
GX = 128
NY = 128
NZ = 64


def draw_image(key, part):
    key = jax.random.fold_in(key, 11)
    noise_key = jax.random.fold_in(key, 0)
    values = jax.random.truncated_normal(noise_key, -3.9, 3.9, (COLS + 1, NZ, NY, GX), jnp.float32)
    return (values[1:] + 0.6 * values[:-1]).astype(jnp.bfloat16)


def draw_picked(key, part):
    key = jax.random.fold_in(key, 23)
    return jax.random.permutation(key, COLS)[:RECYCLE].astype(jnp.int32)


def box_field(key, column):
    column_key = jax.random.fold_in(key, column)
    raw_values = jax.random.randint(column_key, (NZ + 8, NY + 8, GX + 8), -8, 9).astype(jnp.float32)
    along_z = raw_values[0:NZ]
    for offset in range(1, 9):
        along_z = along_z + raw_values[offset:offset + NZ]
    along_y = along_z[:, 0:NY]
    for offset in range(1, 9):
        along_y = along_y + along_z[:, offset:offset + NY]
    along_x = along_y[:, :, 0:GX]
    for offset in range(1, 9):
        along_x = along_x + along_y[:, :, offset:offset + GX]
    return along_x


def draw_basis(key, part):
    key = jax.random.fold_in(key, 31)
    field_key = jax.random.fold_in(key, 0)
    unit_scale = 0.0012966
    factors = jnp.full((COLS,), unit_scale, jnp.float32)
    first = box_field(field_key, 0)

    def advance(previous, inputs):
        column, factor = inputs
        current = box_field(field_key, column)
        mixed = (current * 5.0 + previous * 3.0) * factor
        return (current, jnp.clip(mixed, -6.0, 6.0).astype(jnp.bfloat16))
    columns_index = jnp.arange(1, COLS + 1).astype(jnp.int32)
    _, result = lax.scan(advance, first, (columns_index, factors))
    return result


def draw_material(key, part):
    key = jax.random.fold_in(key, 41)
    which_key, kind_key = jax.random.split(key)
    which = jax.random.randint(which_key, (NZ, NY, GX), 0, 10)
    other = jax.random.randint(kind_key, (NZ, NY, GX), 1, 4)
    return jnp.where(which == 0, other, 0).astype(jnp.int32)


def setup_inputs(seed: int = 0) -> dict:
    key_list = jax.random.split(jax.random.key(seed), 5)
    basis = draw_basis(jax.random.fold_in(key_list[4], 71), 0)
    image = draw_image(jax.random.fold_in(key_list[4], 71), 0)
    material = draw_material(jax.random.fold_in(key_list[4], 71), 0)
    picked = draw_picked(jax.random.fold_in(key_list[4], 71), 0)
    return {"basis": basis, "image": image, "material": material, "picked": picked}


def squared_wave(material):
    return jnp.where(material == 0, 0.3, jnp.where(material == 1, 0.9, jnp.where(material == 2, 1.6, 2.5))).astype(jnp.float32)

def stencil(padded, material):
    padded = jnp.pad(padded, ((0, 0), (0, 0), (0, 0), (1, 1)))
    center = padded[:, 1:-1, 1:-1, 1:-1]
    beside = padded[:, 2:, 1:-1, 1:-1] + padded[:, :-2, 1:-1, 1:-1]
    beside = beside + padded[:, 1:-1, 2:, 1:-1] + padded[:, 1:-1, :-2, 1:-1]
    beside = beside + padded[:, 1:-1, 1:-1, 2:] + padded[:, 1:-1, 1:-1, :-2]
    return (6.0 - squared_wave(material)) * center - beside

def harmonic_columns(gram_matrix, cross_matrix, picked):
    lower_factor = jnp.linalg.cholesky(gram_matrix)
    halfway = lax.linalg.triangular_solve(lower_factor, cross_matrix, left_side=True, lower=True)
    coefficients = lax.linalg.triangular_solve(lower_factor, halfway, left_side=True, lower=True, transpose_a=True)
    return jnp.take(coefficients, picked, axis=1).astype(jnp.bfloat16)

def inverse_factor(normal_matrix):
    lower_factor = jnp.linalg.cholesky(normal_matrix)
    identity = jnp.eye(normal_matrix.shape[0], dtype=normal_matrix.dtype)
    return lax.linalg.triangular_solve(lower_factor, identity, left_side=True, lower=True)

def reference(basis, image, material, picked):
    flat_basis = basis.reshape(COLS, -1)
    flat_image = image.reshape(COLS, -1)
    gram_matrix = jnp.dot(flat_image.astype(jnp.float32), flat_image.T.astype(jnp.float32), preferred_element_type=jnp.float32)
    cross_matrix = jnp.dot(flat_image.astype(jnp.float32), flat_basis.T.astype(jnp.float32), preferred_element_type=jnp.float32)
    chosen = harmonic_columns(gram_matrix, cross_matrix, picked)
    recycle = jnp.dot(chosen.T.astype(jnp.float32), flat_basis.astype(jnp.float32), preferred_element_type=jnp.float32).reshape(RECYCLE, NZ, NY, GX)
    padded = jnp.pad(recycle, ((0, 0), (1, 1), (1, 1), (0, 0)))
    applied = stencil(padded, material)
    flat_applied = applied.reshape(RECYCLE, -1)
    flat_recycle = recycle.reshape(RECYCLE, -1)
    normal_matrix = jnp.dot(flat_applied.astype(jnp.float32), flat_applied.T.astype(jnp.float32), precision=lax.Precision.HIGHEST, preferred_element_type=jnp.float32) / (NZ * NY * GX)
    inverse = inverse_factor(normal_matrix)
    recycle_out = jnp.dot(inverse.astype(jnp.float32), flat_recycle.astype(jnp.float32), precision=lax.Precision.HIGHEST, preferred_element_type=jnp.float32)
    images_out = jnp.dot(inverse.astype(jnp.float32), flat_applied.astype(jnp.float32), precision=lax.Precision.HIGHEST, preferred_element_type=jnp.float32)
    return (recycle_out.reshape(RECYCLE, NZ, NY, GX), images_out.reshape(RECYCLE, NZ, NY, GX))
```

```python
import functools

import jax
import jax.numpy as jnp
from jax import lax
from jax.experimental import pallas as pl
from jax.experimental.pallas import tpu as pltpu
from jax.sharding import PartitionSpec as P

MESH = pl.DeviceIdType.MESH
F32 = jnp.float32
BF16 = jnp.bfloat16
GROUP = 8
PITCH = 40
LANES = 128


def dot_nt(a, b):
    return lax.dot_general(a, b, (((1,), (1,)), ((), ())), preferred_element_type=F32)


def split(value):
    high = value.astype(BF16)
    return high, (value - high.astype(F32)).astype(BF16)


def splat(tile, column):
    return jnp.broadcast_to(tile[:, column:column + 1], tile.shape)


def row_of(tile, index):
    return jnp.broadcast_to(tile[index:index + 1, :], tile.shape)


def merge_rows(tile, rows, first):
    index = lax.broadcasted_iota(jnp.int32, tile.shape, 0)
    for offset, row in enumerate(rows):
        tile = jnp.where(index == first + offset, row, tile)
    return tile


def pivot_block(tiles, step):
    block, first = step // 2, 4 * (step % 2)
    columns = [[splat(tile, 4 * step + j) for j in range(4)] for tile in tiles]
    rows = [row_of(tiles[block], first + i) for i in range(4)]
    pivots = [[row_of(columns[block][j], first + i) for j in range(4)] for i in range(4)]
    return block, first, columns, rows, pivots


def solve_spd(tiles, unknowns):
    for step in range(unknowns // 4):
        block, first, columns, rows, pivots = pivot_block(tiles, step)
        for j in range(4):
            scale = 1.0 / pivots[j][j]
            rows[j] = rows[j] * scale
            for c in range(j + 1, 4):
                pivots[j][c] = pivots[j][c] * scale
            for i in range(4):
                if i != j:
                    factor = pivots[i][j]
                    rows[i] = rows[i] - factor * rows[j]
                    for c in range(j + 1, 4):
                        pivots[i][c] = pivots[i][c] - factor * pivots[j][c]
        updated = []
        for t, tile in enumerate(tiles):
            for j in range(4):
                tile = tile - columns[t][j] * rows[j]
            if t == block:
                tile = merge_rows(tile, rows, first)
            updated.append(tile)
        tiles = updated
    return tiles


def eliminate(tiles, unknowns):
    for step in range(unknowns // 4):
        block, first, columns, rows, pivots = pivot_block(tiles, step)
        done = []
        for j in range(4):
            scale = 1.0 / pivots[j][j]
            done.append(rows[j] * lax.rsqrt(pivots[j][j]))
            rows[j] = rows[j] * scale
            for c in range(j + 1, 4):
                pivots[j][c] = pivots[j][c] * scale
            for i in range(4):
                if i != j:
                    factor = pivots[i][j]
                    rows[i] = rows[i] - factor * rows[j]
                    for c in range(j + 1, 4):
                        pivots[i][c] = pivots[i][c] - factor * pivots[j][c]
        index = lax.broadcasted_iota(jnp.int32, tiles[0].shape, 0)
        updated = []
        for t, tile in enumerate(tiles):
            if t < block:
                updated.append(tile)
                continue
            changed = tile
            for j in range(4):
                changed = changed - columns[t][j] * rows[j]
            if t == block:
                changed = jnp.where(index >= first + 4, changed, tile)
                changed = merge_rows(changed, done, first)
            updated.append(changed)
        tiles = updated
    return tiles


def all_sum(part, slots, gathered, total, sems, slabs, pencils):
    slab, pencil = lax.axis_index("slab"), lax.axis_index("pencil")
    scatter_send, scatter_recv, slab_send, slab_recv, back_send, back_recv = sems
    rows = part.shape[0] // pencils

    def chunk(index):
        return pl.ds(pl.multiple_of(index * rows, rows), rows)

    copies = []
    for d in range(1, pencils):
        peer = lax.rem(pencil + d, pencils)
        copies.append(pltpu.make_async_remote_copy(
            src_ref=part.at[chunk(peer)], dst_ref=slots.at[d - 1],
            send_sem=scatter_send.at[d - 1], recv_sem=scatter_recv.at[d - 1],
            device_id={"slab": slab, "pencil": peer}, device_id_type=MESH))
    for copy in copies:
        copy.start()
    mine = part[chunk(pencil), :]
    for d, copy in enumerate(copies):
        copy.wait_recv()
        mine = mine + slots[d]
    gathered[slab] = mine
    slab_copies = []
    for d in range(1, slabs):
        peer = lax.rem(slab + d, slabs)
        slab_copies.append(pltpu.make_async_remote_copy(
            src_ref=gathered.at[slab], dst_ref=gathered.at[slab],
            send_sem=slab_send.at[d - 1], recv_sem=slab_recv.at[d - 1],
            device_id={"slab": peer, "pencil": pencil}, device_id_type=MESH))
    for copy in slab_copies:
        copy.start()
    for copy in slab_copies:
        copy.wait_recv()
    summed = gathered[0]
    for s in range(1, slabs):
        summed = summed + gathered[s]
    total[chunk(pencil), :] = summed
    back_copies = []
    for d in range(1, pencils):
        peer = lax.rem(pencil + d, pencils)
        back_copies.append(pltpu.make_async_remote_copy(
            src_ref=total.at[chunk(pencil)], dst_ref=total.at[chunk(pencil)],
            send_sem=back_send.at[d - 1], recv_sem=back_recv.at[d - 1],
            device_id={"slab": slab, "pencil": peer}, device_id_type=MESH))
    for copy in back_copies:
        copy.start()
    for copy in back_copies:
        copy.wait_recv()
    for copy in copies + slab_copies + back_copies:
        copy.wait_send()


def main_kernel(
    slabs, pencils, count, cells,
    basis_ref, image_ref, material_ref, picked_ref,
    rec_out, app_out, inverse_out,
    basis_in, image_in, wide, rows_of_basis, weights, rec, app, factor,
    z_send, z_halo, y_send, y_halo,
    part1, slots1, gathered1, total1, part2, slots2, gathered2, total2, turned,
    in_sems, out_sems, halo_send, halo_recv, *sum_sems,
):
    columns, depth, height, width = basis_in.shape[1], *basis_in.shape[:1], *basis_in.shape[2:]
    groups = height // GROUP
    slab, pencil = lax.axis_index("slab"), lax.axis_index("pencil")

    loads = []
    for z in range(depth):
        for which, (source, target) in enumerate(((basis_ref, basis_in), (image_ref, image_in))):
            loads.append(pltpu.make_async_copy(
                source.at[:, z], target.at[z], in_sems.at[2 * z + which]))
    for load in loads:
        load.start()

    barrier = pltpu.get_barrier_semaphore()
    for d in range(1, pencils):
        pl.semaphore_signal(
            barrier, inc=1, device_id={"slab": slab, "pencil": lax.rem(pencil + d, pencils)},
            device_id_type=MESH)
    for d in range(1, slabs):
        pl.semaphore_signal(
            barrier, inc=1, device_id={"slab": lax.rem(slab + d, slabs), "pencil": pencil},
            device_id_type=MESH)

    material = material_ref[...]
    factor[...] = 6.0 - jnp.where(
        material == 0, 0.3,
        jnp.where(material == 1, 0.9, jnp.where(material == 2, 1.6, 2.5))).astype(F32)

    extra = 16 - columns % 16 if columns % 16 else 0
    low = columns - extra
    flat = wide.reshape(2 * columns * PITCH, width)
    gram = jnp.zeros((columns + extra, 2 * columns), F32)
    for z in range(depth):
        loads[2 * z].wait()
        wide[0:columns, 0:height, :] = basis_in[z].astype(F32)
        loads[2 * z + 1].wait()
        wide[columns:2 * columns, 0:height, :] = image_in[z].astype(F32)
        for g in range(groups):
            turned_rows = []
            for y in range(g * GROUP, (g + 1) * GROUP):
                both = flat[pl.ds(y, 2 * columns, stride=PITCH), :].astype(BF16)
                rows_of_basis[z, y] = both[0:columns + extra]
                turned_rows.append(both)
            stacked = jnp.concatenate(turned_rows, axis=1)
            gram = gram + dot_nt(stacked[low:], stacked)

    source_row = lax.broadcasted_iota(jnp.int32, (2 * columns, LANES), 0)
    lane = lax.broadcasted_iota(jnp.int32, (2 * columns, LANES), 1)
    wanted = jnp.where(
        lane < columns, lane + columns, jnp.broadcast_to(picked_ref[...], (2 * columns, LANES)))
    select = jnp.where(source_row == wanted, 1.0, 0.0).astype(BF16)
    high, rest = gram.astype(BF16), gram
    augmented = jnp.dot(high, select, preferred_element_type=F32)
    for _ in range(2):
        rest = rest - high.astype(F32)
        high = rest.astype(BF16)
        augmented = augmented + jnp.dot(high, select, preferred_element_type=F32)
    part1[...] = augmented

    pl.semaphore_wait(barrier, slabs + pencils - 2)
    all_sum(part1, slots1, gathered1, total1, sum_sems[0:6], slabs, pencils)

    tiles = [total1[extra + 8 * t:extra + 8 * (t + 1), :] for t in range(columns // 8)]
    tiles = solve_spd(tiles, columns)
    turned[...] = jnp.zeros_like(turned)
    for t, tile in enumerate(tiles):
        turned[8 * t:8 * (t + 1), :] = tile
    weights[...] = turned[...].T[columns:columns + count, 0:columns + extra].astype(BF16)

    def recycle_layer(z):
        for g in range(groups):
            cells_in = jnp.concatenate(
                [rows_of_basis[z, y] for y in range(g * GROUP, (g + 1) * GROUP)], axis=1)
            result = jnp.dot(weights[...], cells_in, preferred_element_type=F32)
            for i in range(GROUP):
                rec[z + 1, 1 + g * GROUP + i] = result[:, i * width:(i + 1) * width]

    def z_copy(side, peer):
        return pltpu.make_async_remote_copy(
            src_ref=z_send.at[side], dst_ref=z_halo.at[side],
            send_sem=halo_send.at[side], recv_sem=halo_recv.at[side],
            device_id={"slab": peer, "pencil": pencil}, device_id_type=MESH)

    def y_copy(side, peer):
        return pltpu.make_async_remote_copy(
            src_ref=y_send.at[side], dst_ref=y_halo.at[side],
            send_sem=halo_send.at[2 + side], recv_sem=halo_recv.at[2 + side],
            device_id={"slab": slab, "pencil": peer}, device_id_type=MESH)

    z_copies = (z_copy(0, lax.rem(slab + 1, slabs)), z_copy(1, lax.rem(slab + slabs - 1, slabs)))
    y_copies = (y_copy(0, lax.rem(pencil + 1, pencils)),
                y_copy(1, lax.rem(pencil + pencils - 1, pencils)))
    sends = (slab < slabs - 1, slab > 0, pencil < pencils - 1, pencil > 0)
    takes = (slab > 0, slab < slabs - 1, pencil > 0, pencil < pencils - 1)

    recycle_layer(depth - 1)
    z_send[0] = rec[depth, 1:height + 1].astype(BF16)
    pl.when(sends[0])(z_copies[0].start)
    recycle_layer(0)
    z_send[1] = rec[1, 1:height + 1].astype(BF16)
    pl.when(sends[1])(z_copies[1].start)
    pl.loop(1, depth - 1)(recycle_layer)
    y_send[0] = rec[1:depth + 1, height].astype(BF16)
    pl.when(sends[2])(y_copies[0].start)
    y_send[1] = rec[1:depth + 1, 1].astype(BF16)
    pl.when(sends[3])(y_copies[1].start)
    rec_store = pltpu.make_async_copy(
        rec.at[pl.ds(1, depth), pl.ds(1, height)], rec_out, out_sems.at[0])
    rec_store.start()

    lanes = lax.broadcasted_iota(jnp.int32, (count, width), 1)

    def applied_layer(z, normal):
        for g in range(groups):
            values = []
            for y in range(g * GROUP, (g + 1) * GROUP):
                center = rec[z + 1, y + 1]
                beside = rec[z, y + 1] + rec[z + 2, y + 1] + rec[z + 1, y] + rec[z + 1, y + 2]
                beside = beside + jnp.where(lanes == 0, 0.0, pltpu.roll(center, 1, 1))
                beside = beside + jnp.where(
                    lanes == width - 1, 0.0, pltpu.roll(center, width - 1, 1))
                value = factor[z, y:y + 1, :] * center - beside
                app[z, y] = value
                values.append(value)
            high, rest = split(jnp.concatenate(values, axis=1))
            both = jnp.concatenate([high, rest], axis=0)
            normal = normal + dot_nt(both, both)
        return normal

    for side, (take, send) in enumerate(zip(takes[2:], sends[2:])):
        pl.when(take)(y_copies[side].wait_recv)

        @pl.when(jnp.logical_not(take))
        def _():
            y_halo[side] = jnp.zeros(y_halo.shape[1:], BF16)

        rec[1:depth + 1, 0 if side == 0 else height + 1] = y_halo[side].astype(F32)
    normal = lax.fori_loop(1, depth - 1, applied_layer, jnp.zeros((2 * count, 2 * count), F32))
    for side, take in enumerate(takes[:2]):
        pl.when(take)(z_copies[side].wait_recv)

        @pl.when(jnp.logical_not(take))
        def _():
            z_halo[side] = jnp.zeros(z_halo.shape[1:], BF16)

        rec[0 if side == 0 else depth + 1, 1:height + 1] = z_halo[side].astype(F32)
        normal = applied_layer(0 if side == 0 else depth - 1, normal)
    app_store = pltpu.make_async_copy(app, app_out, out_sems.at[1])
    app_store.start()

    turned[0:2 * count, 0:2 * count] = normal
    halves = turned[0:count, :] + turned[count:2 * count, :]
    part2[...] = halves + pltpu.roll(halves, LANES - count, 1)
    all_sum(part2, slots2, gathered2, total2, sum_sems[6:12], slabs, pencils)

    row = lax.broadcasted_iota(jnp.int32, (count, LANES), 0)
    lane = lax.broadcasted_iota(jnp.int32, (count, LANES), 1)
    matrix = jnp.where(
        lane < count, total2[...] * (1.0 / cells), jnp.where(lane == row + count, 1.0, 0.0))
    tiles = eliminate([matrix[8 * t:8 * (t + 1), :] for t in range(count // 8)], count)
    inverse = pltpu.roll(jnp.concatenate(tiles, axis=0), LANES - count, 1)
    inverse = jnp.where(lane <= row, inverse, 0.0)
    high = inverse.astype(BF16).astype(F32)
    rest = (inverse - high).astype(BF16).astype(F32)
    inverse_out[...] = high + pltpu.roll(high, count, 1) + pltpu.roll(rest, 2 * count, 1)

    for copy, send in zip(z_copies + y_copies, sends):
        pl.when(send)(copy.wait_send)
    rec_store.wait()
    app_store.wait()


def final_kernel(inverse_ref, rec_ref, app_ref, rec_out, app_out):
    height, count, width = rec_ref.shape
    factors = inverse_ref[...][:, 0:3 * count].astype(BF16)
    for source, target in ((rec_ref, rec_out), (app_ref, app_out)):
        flat = target.reshape(count * height, width)
        for g in range(height // GROUP):
            values = jnp.concatenate(
                [source[y] for y in range(g * GROUP, (g + 1) * GROUP)], axis=1)
            high, rest = split(values)
            result = jnp.dot(
                factors, jnp.concatenate([high, rest, high], axis=0), preferred_element_type=F32)
            for i in range(GROUP):
                flat[pl.ds(g * GROUP + i, count, stride=height), :] = (
                    result[:, i * width:(i + 1) * width])


def local(slabs, pencils, basis, image, material, picked):
    columns, depth, height, width = basis.shape
    count = picked.shape[0]
    extra = 16 - columns % 16 if columns % 16 else 0
    padded = columns + extra
    cells = depth * height * width * slabs * pencils
    lanes = jnp.pad(
        picked[None, :], ((0, 0), (columns, LANES - columns - count)), constant_values=-1)

    def sum_scratch(rows):
        return [
            pltpu.VMEM((rows, LANES), F32),
            pltpu.VMEM((pencils - 1, rows // pencils, LANES), F32),
            pltpu.VMEM((slabs, rows // pencils, LANES), F32),
            pltpu.VMEM((rows, LANES), F32),
        ]

    def sum_sems():
        return [pltpu.SemaphoreType.DMA((n - 1,)) for n in (
            pencils, pencils, slabs, slabs, pencils, pencils)]

    in_vmem = pl.BlockSpec(memory_space=pltpu.VMEM)
    anywhere = pl.BlockSpec(memory_space=pl.ANY)
    turned_shape = jax.ShapeDtypeStruct((depth, height, count, width), F32)
    rec, app, inverse = pl.pallas_call(
        functools.partial(main_kernel, slabs, pencils, count, cells),
        out_shape=(turned_shape, turned_shape, jax.ShapeDtypeStruct((count, LANES), F32)),
        in_specs=[anywhere, anywhere, in_vmem, in_vmem],
        out_specs=(anywhere, anywhere, in_vmem),
        scratch_shapes=[
            pltpu.VMEM((depth, columns, height, width), BF16),
            pltpu.VMEM((depth, columns, height, width), BF16),
            pltpu.VMEM((2 * columns, PITCH, width), F32),
            pltpu.VMEM((depth, height, padded, width), BF16),
            pltpu.VMEM((count, padded), BF16),
            pltpu.VMEM((depth + 2, height + 2, count, width), F32),
            pltpu.VMEM((depth, height, count, width), F32),
            pltpu.VMEM((depth, height, width), F32),
            pltpu.VMEM((2, height, count, width), BF16),
            pltpu.VMEM((2, height, count, width), BF16),
            pltpu.VMEM((2, depth, count, width), BF16),
            pltpu.VMEM((2, depth, count, width), BF16),
            *sum_scratch(padded),
            *sum_scratch(count),
            pltpu.VMEM((LANES, LANES), F32),
            pltpu.SemaphoreType.DMA((2 * depth,)),
            pltpu.SemaphoreType.DMA((2,)),
            pltpu.SemaphoreType.DMA((4,)),
            pltpu.SemaphoreType.DMA((4,)),
            *sum_sems(),
            *sum_sems(),
        ],
        compiler_params=pltpu.CompilerParams(
            collective_id=0, has_side_effects=True, vmem_limit_bytes=56 * 1024 * 1024),
        name="recycle_update",
    )(basis, image, material, lanes)
    whole = pl.BlockSpec((None, height, count, width), lambda z: (z, 0, 0, 0))
    placed = pl.BlockSpec((count, None, height, width), lambda z: (0, z, 0, 0))
    out = jax.ShapeDtypeStruct((count, depth, height, width), F32)
    return pl.pallas_call(
        final_kernel,
        grid=(depth,),
        out_shape=(out, out),
        in_specs=[pl.BlockSpec((count, LANES), lambda z: (0, 0)), whole, whole],
        out_specs=(placed, placed),
        compiler_params=pltpu.CompilerParams(vmem_limit_bytes=32 * 1024 * 1024),
        name="times_inverse",
    )(inverse, rec, app)


def solution(mesh):
    placed = (
        P(None, "slab", "pencil", None),
        P(None, "slab", "pencil", None),
        P("slab", "pencil", None),
        P(),
    )
    return jax.shard_map(
        functools.partial(local, mesh.shape["slab"], mesh.shape["pencil"]),
        mesh=mesh,
        in_specs=placed,
        out_specs=(P(None, "slab", "pencil", None), P(None, "slab", "pencil", None)),
        check_vma=False,
    )
```

```python
import functools

import jax
import jax.numpy as jnp
from jax import lax
from jax.experimental import pallas as pl
from jax.experimental.pallas import tpu as pltpu
from jax.sharding import PartitionSpec as P

MESH = pl.DeviceIdType.MESH
F32 = jnp.float32
BF16 = jnp.bfloat16
GROUP = 8
PITCH_EXTRA = 1
LANES = 128


def dot_nt(a, b):
    return lax.dot_general(a, b, (((1,), (1,)), ((), ())), preferred_element_type=F32)


def split(value):
    high = value.astype(BF16)
    return high, (value - high.astype(F32)).astype(BF16)


def splat(tile, column):
    return jnp.broadcast_to(tile[:, column:column + 1], tile.shape)


def row_of(tile, index):
    return jnp.broadcast_to(tile[index:index + 1, :], tile.shape)


def merge_rows(tile, rows, first):
    index = lax.broadcasted_iota(jnp.int32, tile.shape, 0)
    for offset, row in enumerate(rows):
        tile = jnp.where(index == first + offset, row, tile)
    return tile


def pivot_block(tiles, step):
    block, first = step // 2, 4 * (step % 2)
    columns = [[splat(tile, 4 * step + j) for j in range(4)] for tile in tiles]
    rows = [row_of(tiles[block], first + i) for i in range(4)]
    pivots = [[row_of(columns[block][j], first + i) for j in range(4)] for i in range(4)]
    return block, first, columns, rows, pivots


def solve_spd(tiles, unknowns):
    for step in range(unknowns // 4):
        block, first, columns, rows, pivots = pivot_block(tiles, step)
        for j in range(4):
            scale = 1.0 / pivots[j][j]
            rows[j] = rows[j] * scale
            for c in range(j + 1, 4):
                pivots[j][c] = pivots[j][c] * scale
            for i in range(4):
                if i != j:
                    factor = pivots[i][j]
                    rows[i] = rows[i] - factor * rows[j]
                    for c in range(j + 1, 4):
                        pivots[i][c] = pivots[i][c] - factor * pivots[j][c]
        updated = []
        for t, tile in enumerate(tiles):
            for j in range(4):
                tile = tile - columns[t][j] * rows[j]
            if t == block:
                tile = merge_rows(tile, rows, first)
            updated.append(tile)
        tiles = updated
    return tiles


def eliminate(tiles, unknowns):
    for step in range(unknowns // 4):
        block, first, columns, rows, pivots = pivot_block(tiles, step)
        done = []
        for j in range(4):
            scale = 1.0 / pivots[j][j]
            done.append(rows[j] * lax.rsqrt(pivots[j][j]))
            rows[j] = rows[j] * scale
            for c in range(j + 1, 4):
                pivots[j][c] = pivots[j][c] * scale
            for i in range(4):
                if i != j:
                    factor = pivots[i][j]
                    rows[i] = rows[i] - factor * rows[j]
                    for c in range(j + 1, 4):
                        pivots[i][c] = pivots[i][c] - factor * pivots[j][c]
        index = lax.broadcasted_iota(jnp.int32, tiles[0].shape, 0)
        updated = []
        for t, tile in enumerate(tiles):
            if t < block:
                updated.append(tile)
                continue
            changed = tile
            for j in range(4):
                changed = changed - columns[t][j] * rows[j]
            if t == block:
                changed = jnp.where(index >= first + 4, changed, tile)
                changed = merge_rows(changed, done, first)
            updated.append(changed)
        tiles = updated
    return tiles


def all_sum(part, slots, gathered, total, sems, slabs, pencils):
    slab, pencil = lax.axis_index("slab"), lax.axis_index("pencil")
    scatter_send, scatter_recv, slab_send, slab_recv, back_send, back_recv = sems
    rows = part.shape[0] // pencils

    def chunk(index):
        return pl.ds(pl.multiple_of(index * rows, rows), rows)

    copies = []
    for d in range(1, pencils):
        peer = lax.rem(pencil + d, pencils)
        copies.append(pltpu.make_async_remote_copy(
            src_ref=part.at[chunk(peer)], dst_ref=slots.at[d - 1],
            send_sem=scatter_send.at[d - 1], recv_sem=scatter_recv.at[d - 1],
            device_id={"slab": slab, "pencil": peer}, device_id_type=MESH))
    for copy in copies:
        copy.start()
    mine = part[chunk(pencil), :]
    for d, copy in enumerate(copies):
        copy.wait_recv()
        mine = mine + slots[d]
    gathered[slab] = mine
    slab_copies = []
    for d in range(1, slabs):
        peer = lax.rem(slab + d, slabs)
        slab_copies.append(pltpu.make_async_remote_copy(
            src_ref=gathered.at[slab], dst_ref=gathered.at[slab],
            send_sem=slab_send.at[d - 1], recv_sem=slab_recv.at[d - 1],
            device_id={"slab": peer, "pencil": pencil}, device_id_type=MESH))
    for copy in slab_copies:
        copy.start()
    for copy in slab_copies:
        copy.wait_recv()
    summed = gathered[0]
    for s in range(1, slabs):
        summed = summed + gathered[s]
    total[chunk(pencil), :] = summed
    back_copies = []
    for d in range(1, pencils):
        peer = lax.rem(pencil + d, pencils)
        back_copies.append(pltpu.make_async_remote_copy(
            src_ref=total.at[chunk(pencil)], dst_ref=total.at[chunk(pencil)],
            send_sem=back_send.at[d - 1], recv_sem=back_recv.at[d - 1],
            device_id={"slab": slab, "pencil": peer}, device_id_type=MESH))
    for copy in back_copies:
        copy.start()
    for copy in back_copies:
        copy.wait_recv()
    for copy in copies + slab_copies + back_copies:
        copy.wait_send()


def main_kernel(
    slabs, pencils, count, cells,
    basis_ref, image_ref, material_ref, picked_ref,
    rec_out, app_out, inverse_out,
    basis_in, image_in, wide, rows_of_basis, weights, rec, app, factor,
    z_send, z_halo, y_send, y_halo,
    part1, slots1, gathered1, total1, part2, slots2, gathered2, total2, turned,
    in_sems, out_sems, halo_send, halo_recv, *sum_sems,
):
    columns, depth, height, width = basis_in.shape[1], *basis_in.shape[:1], *basis_in.shape[2:]
    groups = height // GROUP
    slab, pencil = lax.axis_index("slab"), lax.axis_index("pencil")

    loads = []
    for z in range(depth):
        for which, (source, target) in enumerate(((basis_ref, basis_in), (image_ref, image_in))):
            loads.append(pltpu.make_async_copy(
                source.at[:, z], target.at[z], in_sems.at[2 * z + which]))
    for load in loads:
        load.start()

    barrier = pltpu.get_barrier_semaphore()
    for d in range(1, pencils):
        pl.semaphore_signal(
            barrier, inc=1, device_id={"slab": slab, "pencil": lax.rem(pencil + d, pencils)},
            device_id_type=MESH)
    for d in range(1, slabs):
        pl.semaphore_signal(
            barrier, inc=1, device_id={"slab": lax.rem(slab + d, slabs), "pencil": pencil},
            device_id_type=MESH)

    material = material_ref[...]
    factor[...] = 6.0 - jnp.where(
        material == 0, 0.3,
        jnp.where(material == 1, 0.9, jnp.where(material == 2, 1.6, 2.5))).astype(F32)

    extra = 16 - columns % 16 if columns % 16 else 0
    low = columns - extra
    pitch = height + PITCH_EXTRA

    def gram_layer(z, gram):
        for which, (source, target) in enumerate(((basis_ref, basis_in), (image_ref, image_in))):
            pltpu.make_async_copy(
                source.at[:, z], target.at[z], in_sems.at[2 * z + which]).wait()
            for c in range(columns):
                wide[pl.ds((which * columns + c) * pitch, height), :] = target[z, c].astype(F32)
        for g in range(groups):
            turned_rows = []
            for y in range(g * GROUP, (g + 1) * GROUP):
                both = wide[pl.ds(y, 2 * columns, stride=pitch), :].astype(BF16)
                rows_of_basis[z, y] = both[0:columns + extra]
                turned_rows.append(both)
            stacked = jnp.concatenate(turned_rows, axis=1)
            gram = gram + dot_nt(stacked[low:], stacked)
        return gram

    gram = lax.fori_loop(
        0, depth, gram_layer, jnp.zeros((columns + extra, 2 * columns), F32))

    source_row = lax.broadcasted_iota(jnp.int32, (2 * columns, LANES), 0)
    lane = lax.broadcasted_iota(jnp.int32, (2 * columns, LANES), 1)
    column = lax.broadcasted_iota(jnp.int32, (2 * columns, count), 0)
    chosen_one = jnp.where(column == picked_ref[...], 1.0, 0.0).astype(BF16)
    place = lax.broadcasted_iota(jnp.int32, (count, LANES), 1) - columns
    place = jnp.where(
        place == lax.broadcasted_iota(jnp.int32, (count, LANES), 0), 1.0, 0.0).astype(BF16)
    select = jnp.dot(chosen_one, place, preferred_element_type=F32)
    select = jnp.where(
        jnp.logical_and(lane < columns, source_row == lane + columns), 1.0, select).astype(BF16)
    high, rest = gram.astype(BF16), gram
    augmented = jnp.dot(high, select, preferred_element_type=F32)
    for _ in range(2):
        rest = rest - high.astype(F32)
        high = rest.astype(BF16)
        augmented = augmented + jnp.dot(high, select, preferred_element_type=F32)
    part1[...] = augmented

    pl.semaphore_wait(barrier, slabs + pencils - 2)
    all_sum(part1, slots1, gathered1, total1, sum_sems[0:6], slabs, pencils)

    tiles = [total1[extra + 8 * t:extra + 8 * (t + 1), :] for t in range(columns // 8)]
    tiles = solve_spd(tiles, columns)
    turned[...] = jnp.zeros_like(turned)
    for t, tile in enumerate(tiles):
        turned[8 * t:8 * (t + 1), :] = tile
    weights[...] = turned[...].T[columns:columns + count, 0:columns + extra].astype(BF16)

    def recycle_layer(z):
        for g in range(groups):
            cells_in = jnp.concatenate(
                [rows_of_basis[z, y] for y in range(g * GROUP, (g + 1) * GROUP)], axis=1)
            result = jnp.dot(weights[...], cells_in, preferred_element_type=F32)
            for i in range(GROUP):
                rec[z + 1, 1 + g * GROUP + i] = result[:, i * width:(i + 1) * width]

    def z_copy(side, peer):
        return pltpu.make_async_remote_copy(
            src_ref=z_send.at[side], dst_ref=z_halo.at[side],
            send_sem=halo_send.at[side], recv_sem=halo_recv.at[side],
            device_id={"slab": peer, "pencil": pencil}, device_id_type=MESH)

    def y_copy(side, peer):
        return pltpu.make_async_remote_copy(
            src_ref=y_send.at[side], dst_ref=y_halo.at[side],
            send_sem=halo_send.at[2 + side], recv_sem=halo_recv.at[2 + side],
            device_id={"slab": slab, "pencil": peer}, device_id_type=MESH)

    z_copies = (z_copy(0, lax.rem(slab + 1, slabs)), z_copy(1, lax.rem(slab + slabs - 1, slabs)))
    y_copies = (y_copy(0, lax.rem(pencil + 1, pencils)),
                y_copy(1, lax.rem(pencil + pencils - 1, pencils)))
    sends = (slab < slabs - 1, slab > 0, pencil < pencils - 1, pencil > 0)
    takes = (slab > 0, slab < slabs - 1, pencil > 0, pencil < pencils - 1)

    recycle_layer(depth - 1)
    z_send[0] = rec[depth, 1:height + 1].astype(BF16)
    pl.when(sends[0])(z_copies[0].start)
    recycle_layer(0)
    z_send[1] = rec[1, 1:height + 1].astype(BF16)
    pl.when(sends[1])(z_copies[1].start)
    pl.loop(1, depth - 1)(recycle_layer)
    y_send[0] = rec[1:depth + 1, height].astype(BF16)
    pl.when(sends[2])(y_copies[0].start)
    y_send[1] = rec[1:depth + 1, 1].astype(BF16)
    pl.when(sends[3])(y_copies[1].start)
    rec_store = pltpu.make_async_copy(
        rec.at[pl.ds(1, depth), pl.ds(1, height)], rec_out, out_sems.at[0])
    rec_store.start()

    lanes = lax.broadcasted_iota(jnp.int32, (count, width), 1)

    def applied_layer(z, normal):
        for g in range(groups):
            values = []
            for y in range(g * GROUP, (g + 1) * GROUP):
                center = rec[z + 1, y + 1]
                beside = rec[z, y + 1] + rec[z + 2, y + 1] + rec[z + 1, y] + rec[z + 1, y + 2]
                beside = beside + jnp.where(lanes == 0, 0.0, pltpu.roll(center, 1, 1))
                beside = beside + jnp.where(
                    lanes == width - 1, 0.0, pltpu.roll(center, width - 1, 1))
                value = factor[z, y:y + 1, :] * center - beside
                app[z, y] = value
                values.append(value)
            high, rest = split(jnp.concatenate(values, axis=1))
            both = jnp.concatenate([high, rest], axis=0)
            normal = normal + dot_nt(both, both)
        return normal

    for side, (take, send) in enumerate(zip(takes[2:], sends[2:])):
        pl.when(take)(y_copies[side].wait_recv)

        @pl.when(jnp.logical_not(take))
        def _():
            y_halo[side] = jnp.zeros(y_halo.shape[1:], BF16)

        rec[1:depth + 1, 0 if side == 0 else height + 1] = y_halo[side].astype(F32)
    normal = lax.fori_loop(1, depth - 1, applied_layer, jnp.zeros((2 * count, 2 * count), F32))
    for side, take in enumerate(takes[:2]):
        pl.when(take)(z_copies[side].wait_recv)

        @pl.when(jnp.logical_not(take))
        def _():
            z_halo[side] = jnp.zeros(z_halo.shape[1:], BF16)

        rec[0 if side == 0 else depth + 1, 1:height + 1] = z_halo[side].astype(F32)
        normal = applied_layer(0 if side == 0 else depth - 1, normal)
    app_store = pltpu.make_async_copy(app, app_out, out_sems.at[1])
    app_store.start()

    turned[0:2 * count, 0:2 * count] = normal
    halves = turned[0:count, :] + turned[count:2 * count, :]
    part2[...] = halves + pltpu.roll(halves, LANES - count, 1)
    all_sum(part2, slots2, gathered2, total2, sum_sems[6:12], slabs, pencils)

    row = lax.broadcasted_iota(jnp.int32, (count, LANES), 0)
    lane = lax.broadcasted_iota(jnp.int32, (count, LANES), 1)
    matrix = jnp.where(
        lane < count, total2[...] * (1.0 / cells), jnp.where(lane == row + count, 1.0, 0.0))
    tiles = eliminate([matrix[8 * t:8 * (t + 1), :] for t in range(count // 8)], count)
    inverse = pltpu.roll(jnp.concatenate(tiles, axis=0), LANES - count, 1)
    inverse = jnp.where(lane <= row, inverse, 0.0)
    high = inverse.astype(BF16).astype(F32)
    rest = (inverse - high).astype(BF16).astype(F32)
    inverse_out[...] = high + pltpu.roll(high, count, 1) + pltpu.roll(rest, 2 * count, 1)

    for copy, send in zip(z_copies + y_copies, sends):
        pl.when(send)(copy.wait_send)
    rec_store.wait()
    app_store.wait()


def final_kernel(inverse_ref, rec_ref, app_ref, rec_out, app_out, rec_wide, app_wide):
    height, count, width = rec_ref.shape
    factors = inverse_ref[...][:, 0:3 * count].astype(BF16)
    pitch = height + PITCH_EXTRA
    for source, target, wide in ((rec_ref, rec_out, rec_wide), (app_ref, app_out, app_wide)):
        for g in range(height // GROUP):
            values = jnp.concatenate(
                [source[y] for y in range(g * GROUP, (g + 1) * GROUP)], axis=1)
            high, rest = split(values)
            result = jnp.dot(
                factors, jnp.concatenate([high, rest, high], axis=0), preferred_element_type=F32)
            for i in range(GROUP):
                wide[pl.ds(g * GROUP + i, count, stride=pitch), :] = (
                    result[:, i * width:(i + 1) * width])
        for k in range(count):
            target[k] = wide[pl.ds(k * pitch, height), :]


def local(slabs, pencils, basis, image, material, picked):
    columns, depth, height, width = basis.shape
    count = picked.shape[0]
    extra = 16 - columns % 16 if columns % 16 else 0
    padded = columns + extra
    cells = depth * height * width * slabs * pencils

    def sum_scratch(rows):
        return [
            pltpu.VMEM((rows, LANES), F32),
            pltpu.VMEM((pencils - 1, rows // pencils, LANES), F32),
            pltpu.VMEM((slabs, rows // pencils, LANES), F32),
            pltpu.VMEM((rows, LANES), F32),
        ]

    def sum_sems():
        return [pltpu.SemaphoreType.DMA((n - 1,)) for n in (
            pencils, pencils, slabs, slabs, pencils, pencils)]

    in_vmem = pl.BlockSpec(memory_space=pltpu.VMEM)
    anywhere = pl.BlockSpec(memory_space=pl.ANY)
    turned_shape = jax.ShapeDtypeStruct((depth, height, count, width), F32)
    rec, app, inverse = pl.pallas_call(
        functools.partial(main_kernel, slabs, pencils, count, cells),
        out_shape=(turned_shape, turned_shape, jax.ShapeDtypeStruct((count, LANES), F32)),
        in_specs=[anywhere, anywhere, in_vmem, in_vmem],
        out_specs=(anywhere, anywhere, in_vmem),
        scratch_shapes=[
            pltpu.VMEM((depth, columns, height, width), BF16),
            pltpu.VMEM((depth, columns, height, width), BF16),
            pltpu.VMEM((2 * columns * (height + PITCH_EXTRA), width), F32),
            pltpu.VMEM((depth, height, padded, width), BF16),
            pltpu.VMEM((count, padded), BF16),
            pltpu.VMEM((depth + 2, height + 2, count, width), F32),
            pltpu.VMEM((depth, height, count, width), F32),
            pltpu.VMEM((depth, height, width), F32),
            pltpu.VMEM((2, height, count, width), BF16),
            pltpu.VMEM((2, height, count, width), BF16),
            pltpu.VMEM((2, depth, count, width), BF16),
            pltpu.VMEM((2, depth, count, width), BF16),
            *sum_scratch(padded),
            *sum_scratch(count),
            pltpu.VMEM((LANES, LANES), F32),
            pltpu.SemaphoreType.DMA((2 * depth,)),
            pltpu.SemaphoreType.DMA((2,)),
            pltpu.SemaphoreType.DMA((4,)),
            pltpu.SemaphoreType.DMA((4,)),
            *sum_sems(),
            *sum_sems(),
        ],
        compiler_params=pltpu.CompilerParams(
            collective_id=0, has_side_effects=True, vmem_limit_bytes=56 * 1024 * 1024),
        name="recycle_update",
    )(basis, image, material, picked[None, :])
    whole = pl.BlockSpec((None, height, count, width), lambda z: (z, 0, 0, 0))
    placed = pl.BlockSpec((count, None, height, width), lambda z: (0, z, 0, 0))
    out = jax.ShapeDtypeStruct((count, depth, height, width), F32)
    return pl.pallas_call(
        final_kernel,
        grid=(depth,),
        out_shape=(out, out),
        in_specs=[pl.BlockSpec((count, LANES), lambda z: (0, 0)), whole, whole],
        out_specs=(placed, placed),
        scratch_shapes=[pltpu.VMEM((count * (height + PITCH_EXTRA), width), F32)] * 2,
        compiler_params=pltpu.CompilerParams(vmem_limit_bytes=60 * 1024 * 1024),
        name="times_inverse",
    )(inverse, rec, app)


def solution(mesh):
    placed = (
        P(None, "slab", "pencil", None),
        P(None, "slab", "pencil", None),
        P("slab", "pencil", None),
        P(),
    )
    return jax.shard_map(
        functools.partial(local, mesh.shape["slab"], mesh.shape["pencil"]),
        mesh=mesh,
        in_specs=placed,
        out_specs=(P(None, "slab", "pencil", None), P(None, "slab", "pencil", None)),
        check_vma=False,
    )
```

```python
import functools

import jax
import jax.numpy as jnp
from jax import lax
from jax.experimental import pallas as pl
from jax.experimental.pallas import tpu as pltpu
from jax.sharding import PartitionSpec as P

MESH = pl.DeviceIdType.MESH
F32 = jnp.float32
BF16 = jnp.bfloat16
GROUP = 8
PITCH_EXTRA = 1
LANES = 128


def dot_nt(a, b):
    return lax.dot_general(a, b, (((1,), (1,)), ((), ())), preferred_element_type=F32)


def split(value):
    high = value.astype(BF16)
    return high, (value - high.astype(F32)).astype(BF16)


def reciprocal(value):
    guess = pl.reciprocal(value, approx=True)
    for _ in range(2):
        guess = guess + guess * (1.0 - value * guess)
    return guess


def splat(tile, column):
    return jnp.broadcast_to(tile[:, column:column + 1], tile.shape)


def row_of(tile, index):
    return jnp.broadcast_to(tile[index:index + 1, :], tile.shape)


def merge_rows(tile, rows, first):
    index = lax.broadcasted_iota(jnp.int32, tile.shape, 0)
    for offset, row in enumerate(rows):
        tile = jnp.where(index == first + offset, row, tile)
    return tile


def pivot_block(tiles, step):
    block, first = step // 2, 4 * (step % 2)
    columns = [[splat(tile, 4 * step + j) for j in range(4)] for tile in tiles]
    rows = [row_of(tiles[block], first + i) for i in range(4)]
    pivots = [[row_of(columns[block][j], first + i) for j in range(4)] for i in range(4)]
    return block, first, columns, rows, pivots


def solve_spd(tiles, unknowns):
    for step in range(unknowns // 4):
        block, first, columns, rows, pivots = pivot_block(tiles, step)
        for j in range(4):
            scale = reciprocal(pivots[j][j])
            rows[j] = rows[j] * scale
            for c in range(j + 1, 4):
                pivots[j][c] = pivots[j][c] * scale
            for i in range(4):
                if i != j:
                    factor = pivots[i][j]
                    rows[i] = rows[i] - factor * rows[j]
                    for c in range(j + 1, 4):
                        pivots[i][c] = pivots[i][c] - factor * pivots[j][c]
        updated = []
        for t, tile in enumerate(tiles):
            for j in range(4):
                tile = tile - columns[t][j] * rows[j]
            if t == block:
                tile = merge_rows(tile, rows, first)
            updated.append(tile)
        tiles = updated
    return tiles


def eliminate(tiles, unknowns):
    for step in range(unknowns // 4):
        block, first, columns, rows, pivots = pivot_block(tiles, step)
        done = []
        for j in range(4):
            scale = reciprocal(pivots[j][j])
            done.append(rows[j] * lax.rsqrt(pivots[j][j]))
            rows[j] = rows[j] * scale
            for c in range(j + 1, 4):
                pivots[j][c] = pivots[j][c] * scale
            for i in range(4):
                if i != j:
                    factor = pivots[i][j]
                    rows[i] = rows[i] - factor * rows[j]
                    for c in range(j + 1, 4):
                        pivots[i][c] = pivots[i][c] - factor * pivots[j][c]
        index = lax.broadcasted_iota(jnp.int32, tiles[0].shape, 0)
        updated = []
        for t, tile in enumerate(tiles):
            if t < block:
                updated.append(tile)
                continue
            changed = tile
            for j in range(4):
                changed = changed - columns[t][j] * rows[j]
            if t == block:
                changed = jnp.where(index >= first + 4, changed, tile)
                changed = merge_rows(changed, done, first)
            updated.append(changed)
        tiles = updated
    return tiles


def all_sum(part, slots, gathered, total, sems, slabs, pencils):
    slab, pencil = lax.axis_index("slab"), lax.axis_index("pencil")
    scatter_send, scatter_recv, slab_send, slab_recv, back_send, back_recv = sems
    rows = part.shape[0] // pencils

    def chunk(index):
        return pl.ds(pl.multiple_of(index * rows, rows), rows)

    copies = []
    for d in range(1, pencils):
        peer = lax.rem(pencil + d, pencils)
        copies.append(pltpu.make_async_remote_copy(
            src_ref=part.at[chunk(peer)], dst_ref=slots.at[d - 1],
            send_sem=scatter_send.at[d - 1], recv_sem=scatter_recv.at[d - 1],
            device_id={"slab": slab, "pencil": peer}, device_id_type=MESH))
    for copy in copies:
        copy.start()
    mine = part[chunk(pencil), :]
    for d, copy in enumerate(copies):
        copy.wait_recv()
        mine = mine + slots[d]
    gathered[slab] = mine
    slab_copies = []
    for d in range(1, slabs):
        peer = lax.rem(slab + d, slabs)
        slab_copies.append(pltpu.make_async_remote_copy(
            src_ref=gathered.at[slab], dst_ref=gathered.at[slab],
            send_sem=slab_send.at[d - 1], recv_sem=slab_recv.at[d - 1],
            device_id={"slab": peer, "pencil": pencil}, device_id_type=MESH))
    for copy in slab_copies:
        copy.start()
    for copy in slab_copies:
        copy.wait_recv()
    summed = gathered[0]
    for s in range(1, slabs):
        summed = summed + gathered[s]
    total[chunk(pencil), :] = summed
    back_copies = []
    for d in range(1, pencils):
        peer = lax.rem(pencil + d, pencils)
        back_copies.append(pltpu.make_async_remote_copy(
            src_ref=total.at[chunk(pencil)], dst_ref=total.at[chunk(pencil)],
            send_sem=back_send.at[d - 1], recv_sem=back_recv.at[d - 1],
            device_id={"slab": slab, "pencil": peer}, device_id_type=MESH))
    for copy in back_copies:
        copy.start()
    for copy in back_copies:
        copy.wait_recv()
    for copy in copies + slab_copies + back_copies:
        copy.wait_send()


def gather_sum(value, slots, send, recv, axis, count):
    me = lax.axis_index(axis)
    place = {"slab": lax.axis_index("slab"), "pencil": lax.axis_index("pencil")}
    slots[me] = value
    copies = []
    for d in range(1, count):
        copies.append(pltpu.make_async_remote_copy(
            src_ref=slots.at[me], dst_ref=slots.at[me],
            send_sem=send.at[d - 1], recv_sem=recv.at[d - 1],
            device_id={**place, axis: lax.rem(me + d, count)}, device_id_type=MESH))
    for copy in copies:
        copy.start()
    for copy in copies:
        copy.wait_recv()
    total = slots[0]
    for s in range(1, count):
        total = total + slots[s]
    return total, copies


def main_kernel(
    slabs, pencils, count, cells,
    basis_ref, image_ref, material_ref, picked_ref,
    rec_out, app_out, inverse_out,
    basis_in, image_in, wide, rows_of_basis, weights, rec, rec_halves, app_halves, factor,
    z_send, z_halo, y_send, y_halo,
    part1, slots1, gathered1, total1, slots2, gathered2, turned,
    in_sems, out_sems, halo_send, halo_recv, *sum_sems,
):
    columns, depth, height, width = basis_in.shape[1], *basis_in.shape[:1], *basis_in.shape[2:]
    groups = height // GROUP
    slab, pencil = lax.axis_index("slab"), lax.axis_index("pencil")

    loads = []
    for z in range(depth):
        for which, (source, target) in enumerate(((basis_ref, basis_in), (image_ref, image_in))):
            loads.append(pltpu.make_async_copy(
                source.at[:, z], target.at[z], in_sems.at[2 * z + which]))
    for load in loads:
        load.start()

    barrier = pltpu.get_barrier_semaphore()
    for d in range(1, pencils):
        pl.semaphore_signal(
            barrier, inc=1, device_id={"slab": slab, "pencil": lax.rem(pencil + d, pencils)},
            device_id_type=MESH)
    for d in range(1, slabs):
        pl.semaphore_signal(
            barrier, inc=1, device_id={"slab": lax.rem(slab + d, slabs), "pencil": pencil},
            device_id_type=MESH)

    material = material_ref[...]
    factor[...] = 6.0 - jnp.where(
        material == 0, 0.3,
        jnp.where(material == 1, 0.9, jnp.where(material == 2, 1.6, 2.5))).astype(F32)

    extra = 16 - columns % 16 if columns % 16 else 0
    low = columns - extra
    pitch = height + PITCH_EXTRA

    def gram_layer(z, gram):
        for which, (source, target) in enumerate(((basis_ref, basis_in), (image_ref, image_in))):
            pltpu.make_async_copy(
                source.at[:, z], target.at[z], in_sems.at[2 * z + which]).wait()
            for c in range(columns):
                wide[pl.ds((which * columns + c) * pitch, height), :] = target[z, c].astype(F32)
        for g in range(groups):
            turned_rows = []
            for y in range(g * GROUP, (g + 1) * GROUP):
                both = wide[pl.ds(y, 2 * columns, stride=pitch), :].astype(BF16)
                rows_of_basis[z, y] = both[0:columns + extra]
                turned_rows.append(both)
            stacked = jnp.concatenate(turned_rows, axis=1)
            gram = gram + dot_nt(stacked[low:], stacked)
        return gram

    gram = lax.fori_loop(
        0, depth, gram_layer, jnp.zeros((columns + extra, 2 * columns), F32))

    source_row = lax.broadcasted_iota(jnp.int32, (2 * columns, LANES), 0)
    lane = lax.broadcasted_iota(jnp.int32, (2 * columns, LANES), 1)
    column = lax.broadcasted_iota(jnp.int32, (2 * columns, count), 0)
    chosen_one = jnp.where(column == picked_ref[...], 1.0, 0.0).astype(BF16)
    place = lax.broadcasted_iota(jnp.int32, (count, LANES), 1) - columns
    place = jnp.where(
        place == lax.broadcasted_iota(jnp.int32, (count, LANES), 0), 1.0, 0.0).astype(BF16)
    select = jnp.dot(chosen_one, place, preferred_element_type=F32)
    select = jnp.where(
        jnp.logical_and(lane < columns, source_row == lane + columns), 1.0, select).astype(BF16)
    high, rest = gram.astype(BF16), gram
    augmented = jnp.dot(high, select, preferred_element_type=F32)
    for _ in range(2):
        rest = rest - high.astype(F32)
        high = rest.astype(BF16)
        augmented = augmented + jnp.dot(high, select, preferred_element_type=F32)
    part1[...] = augmented

    pl.semaphore_wait(barrier, slabs + pencils - 2)
    all_sum(part1, slots1, gathered1, total1, sum_sems[0:6], slabs, pencils)

    tiles = [total1[extra + 8 * t:extra + 8 * (t + 1), :] for t in range(columns // 8)]
    tiles = solve_spd(tiles, columns)
    turned[...] = jnp.zeros_like(turned)
    for t, tile in enumerate(tiles):
        turned[8 * t:8 * (t + 1), :] = tile
    weights[...] = turned[...].T[columns:columns + count, 0:columns + extra].astype(BF16)

    def recycle_layer(z):
        for g in range(groups):
            cells_in = jnp.concatenate(
                [rows_of_basis[z, y] for y in range(g * GROUP, (g + 1) * GROUP)], axis=1)
            result = jnp.dot(weights[...], cells_in, preferred_element_type=F32)
            for i in range(GROUP):
                rec[z + 1, 1 + g * GROUP + i] = result[:, i * width:(i + 1) * width]

    def z_copy(side, peer):
        return pltpu.make_async_remote_copy(
            src_ref=z_send.at[side], dst_ref=z_halo.at[side],
            send_sem=halo_send.at[side], recv_sem=halo_recv.at[side],
            device_id={"slab": peer, "pencil": pencil}, device_id_type=MESH)

    def y_copy(side, peer):
        return pltpu.make_async_remote_copy(
            src_ref=y_send.at[side], dst_ref=y_halo.at[side],
            send_sem=halo_send.at[2 + side], recv_sem=halo_recv.at[2 + side],
            device_id={"slab": slab, "pencil": peer}, device_id_type=MESH)

    z_copies = (z_copy(0, lax.rem(slab + 1, slabs)), z_copy(1, lax.rem(slab + slabs - 1, slabs)))
    y_copies = (y_copy(0, lax.rem(pencil + 1, pencils)),
                y_copy(1, lax.rem(pencil + pencils - 1, pencils)))
    sends = (slab < slabs - 1, slab > 0, pencil < pencils - 1, pencil > 0)
    takes = (slab > 0, slab < slabs - 1, pencil > 0, pencil < pencils - 1)

    recycle_layer(depth - 1)
    z_send[0] = rec[depth, 1:height + 1].astype(BF16)
    pl.when(sends[0])(z_copies[0].start)
    recycle_layer(0)
    z_send[1] = rec[1, 1:height + 1].astype(BF16)
    pl.when(sends[1])(z_copies[1].start)
    pl.loop(1, depth - 1)(recycle_layer)
    y_send[0] = rec[1:depth + 1, height].astype(BF16)
    pl.when(sends[2])(y_copies[0].start)
    y_send[1] = rec[1:depth + 1, 1].astype(BF16)
    pl.when(sends[3])(y_copies[1].start)

    lanes = lax.broadcasted_iota(jnp.int32, (count, width), 1)

    def applied_layer(z, normal):
        for g in range(groups):
            values = []
            for y in range(g * GROUP, (g + 1) * GROUP):
                center = rec[z + 1, y + 1]
                beside = rec[z, y + 1] + rec[z + 2, y + 1] + rec[z + 1, y] + rec[z + 1, y + 2]
                beside = beside + jnp.where(lanes == 0, 0.0, pltpu.roll(center, 1, 1))
                beside = beside + jnp.where(
                    lanes == width - 1, 0.0, pltpu.roll(center, width - 1, 1))
                value = factor[z, y:y + 1, :] * center - beside
                values.append(value)
            high, rest = split(jnp.concatenate(values, axis=1))
            both = jnp.concatenate([high, rest], axis=0)
            for i in range(GROUP):
                app_halves[z, g * GROUP + i] = both[:, i * width:(i + 1) * width]
            normal = normal + dot_nt(both, both)
        return normal

    def halve_layer(z):
        for y in range(height):
            high, rest = split(rec[z + 1, y + 1])
            rec_halves[z, y] = jnp.concatenate([high, rest], axis=0)

    for side, (take, send) in enumerate(zip(takes[2:], sends[2:])):
        pl.when(take)(y_copies[side].wait_recv)

        @pl.when(jnp.logical_not(take))
        def _():
            y_halo[side] = jnp.zeros(y_halo.shape[1:], BF16)

        rec[1:depth + 1, 0 if side == 0 else height + 1] = y_halo[side].astype(F32)
    normal = lax.fori_loop(1, depth - 1, applied_layer, jnp.zeros((2 * count, 2 * count), F32))
    pl.loop(0, depth)(halve_layer)
    rec_store = pltpu.make_async_copy(rec_halves, rec_out, out_sems.at[0])
    rec_store.start()
    for side, take in enumerate(takes[:2]):
        pl.when(take)(z_copies[side].wait_recv)

        @pl.when(jnp.logical_not(take))
        def _():
            z_halo[side] = jnp.zeros(z_halo.shape[1:], BF16)

        rec[0 if side == 0 else depth + 1, 1:height + 1] = z_halo[side].astype(F32)
        normal = applied_layer(0 if side == 0 else depth - 1, normal)
    app_store = pltpu.make_async_copy(app_halves, app_out, out_sems.at[1])
    app_store.start()

    turned[0:2 * count, 0:2 * count] = normal
    halves = turned[0:count, :] + turned[count:2 * count, :]
    halves = halves + pltpu.roll(halves, LANES - count, 1)
    lane = lax.broadcasted_iota(jnp.int32, (8, LANES), 1)
    packed = halves[0:8]
    for t in range(1, count // 8):
        packed = jnp.where(
            lane < t * count, packed, pltpu.roll(halves[8 * t:8 * (t + 1)], t * count, 1))
    packed, pencil_copies = gather_sum(
        packed, slots2, sum_sems[6], sum_sems[7], "pencil", pencils)
    packed, slab_copies = gather_sum(
        packed, gathered2, sum_sems[8], sum_sems[9], "slab", slabs)
    total2 = jnp.concatenate(
        [packed] + [pltpu.roll(packed, LANES - t * count, 1) for t in range(1, count // 8)], axis=0)

    row = lax.broadcasted_iota(jnp.int32, (count, LANES), 0)
    lane = lax.broadcasted_iota(jnp.int32, (count, LANES), 1)
    matrix = jnp.where(
        lane < count, total2 * (1.0 / cells), jnp.where(lane == row + count, 1.0, 0.0))
    tiles = eliminate([matrix[8 * t:8 * (t + 1), :] for t in range(count // 8)], count)
    inverse = pltpu.roll(jnp.concatenate(tiles, axis=0), LANES - count, 1)
    inverse = jnp.where(lane <= row, inverse, 0.0)
    high = inverse.astype(BF16).astype(F32)
    rest = (inverse - high).astype(BF16).astype(F32)
    inverse_out[...] = high + pltpu.roll(high, count, 1) + pltpu.roll(rest, 2 * count, 1)

    for copy in pencil_copies + slab_copies:
        copy.wait_send()
    for copy, send in zip(z_copies + y_copies, sends):
        pl.when(send)(copy.wait_send)
    rec_store.wait()
    app_store.wait()


def final_kernel(inverse_ref, rec_ref, app_ref, rec_out, app_out):
    height, count, width = rec_ref.shape[0], rec_ref.shape[1] // 2, rec_ref.shape[2]
    factors = inverse_ref[...][:, 0:3 * count].astype(BF16)
    for source, target in ((rec_ref, rec_out), (app_ref, app_out)):
        flat = target.reshape(count * height, width)
        for g in range(height // GROUP):
            values = jnp.concatenate(
                [source[y] for y in range(g * GROUP, (g + 1) * GROUP)], axis=1)
            result = jnp.dot(
                factors, jnp.concatenate([values, values[0:count]], axis=0),
                preferred_element_type=F32)
            for i in range(GROUP):
                flat[pl.ds(g * GROUP + i, count, stride=height), :] = (
                    result[:, i * width:(i + 1) * width])


def local(slabs, pencils, basis, image, material, picked):
    columns, depth, height, width = basis.shape
    count = picked.shape[0]
    extra = 16 - columns % 16 if columns % 16 else 0
    padded = columns + extra
    cells = depth * height * width * slabs * pencils

    def sum_scratch(rows):
        return [
            pltpu.VMEM((rows, LANES), F32),
            pltpu.VMEM((pencils - 1, rows // pencils, LANES), F32),
            pltpu.VMEM((slabs, rows // pencils, LANES), F32),
            pltpu.VMEM((rows, LANES), F32),
        ]

    def sum_sems(*counts):
        return [pltpu.SemaphoreType.DMA((n - 1,)) for n in counts]

    in_vmem = pl.BlockSpec(memory_space=pltpu.VMEM)
    anywhere = pl.BlockSpec(memory_space=pl.ANY)
    turned_shape = jax.ShapeDtypeStruct((depth, height, 2 * count, width), BF16)
    rec, app, inverse = pl.pallas_call(
        functools.partial(main_kernel, slabs, pencils, count, cells),
        out_shape=(turned_shape, turned_shape, jax.ShapeDtypeStruct((count, LANES), F32)),
        in_specs=[anywhere, anywhere, in_vmem, in_vmem],
        out_specs=(anywhere, anywhere, in_vmem),
        scratch_shapes=[
            pltpu.VMEM((depth, columns, height, width), BF16),
            pltpu.VMEM((depth, columns, height, width), BF16),
            pltpu.VMEM((2 * columns * (height + PITCH_EXTRA), width), F32),
            pltpu.VMEM((depth, height, padded, width), BF16),
            pltpu.VMEM((count, padded), BF16),
            pltpu.VMEM((depth + 2, height + 2, count, width), F32),
            pltpu.VMEM((depth, height, 2 * count, width), BF16),
            pltpu.VMEM((depth, height, 2 * count, width), BF16),
            pltpu.VMEM((depth, height, width), F32),
            pltpu.VMEM((2, height, count, width), BF16),
            pltpu.VMEM((2, height, count, width), BF16),
            pltpu.VMEM((2, depth, count, width), BF16),
            pltpu.VMEM((2, depth, count, width), BF16),
            *sum_scratch(padded),
            pltpu.VMEM((pencils, 8, LANES), F32),
            pltpu.VMEM((slabs, 8, LANES), F32),
            pltpu.VMEM((LANES, LANES), F32),
            pltpu.SemaphoreType.DMA((2 * depth,)),
            pltpu.SemaphoreType.DMA((2,)),
            pltpu.SemaphoreType.DMA((4,)),
            pltpu.SemaphoreType.DMA((4,)),
            *sum_sems(pencils, pencils, slabs, slabs, pencils, pencils),
            *sum_sems(pencils, pencils, slabs, slabs),
        ],
        compiler_params=pltpu.CompilerParams(
            collective_id=0, has_side_effects=True, vmem_limit_bytes=56 * 1024 * 1024),
        name="recycle_update",
    )(basis, image, material, picked[None, :])
    whole = pl.BlockSpec((None, height, 2 * count, width), lambda z: (z, 0, 0, 0))
    placed = pl.BlockSpec((count, None, height, width), lambda z: (0, z, 0, 0))
    out = jax.ShapeDtypeStruct((count, depth, height, width), F32)
    return pl.pallas_call(
        final_kernel,
        grid=(depth,),
        out_shape=(out, out),
        in_specs=[pl.BlockSpec((count, LANES), lambda z: (0, 0)), whole, whole],
        out_specs=(placed, placed),
        compiler_params=pltpu.CompilerParams(vmem_limit_bytes=60 * 1024 * 1024),
        name="times_inverse",
    )(inverse, rec, app)


def solution(mesh):
    placed = (
        P(None, "slab", "pencil", None),
        P(None, "slab", "pencil", None),
        P("slab", "pencil", None),
        P(),
    )
    return jax.shard_map(
        functools.partial(local, mesh.shape["slab"], mesh.shape["pencil"]),
        mesh=mesh,
        in_specs=placed,
        out_specs=(P(None, "slab", "pencil", None), P(None, "slab", "pencil", None)),
        check_vma=False,
    )
```

```python
import functools

import jax
import jax.numpy as jnp
from jax import lax
from jax.experimental import pallas as pl
from jax.experimental.pallas import tpu as pltpu
from jax.sharding import PartitionSpec as P

MESH = pl.DeviceIdType.MESH
F32 = jnp.float32
BF16 = jnp.bfloat16
GROUP = 8
PITCH_EXTRA = 1
LANES = 128


def dot_nt(a, b):
    return lax.dot_general(a, b, (((1,), (1,)), ((), ())), preferred_element_type=F32)


def split(value):
    high = value.astype(BF16)
    return high, (value - high.astype(F32)).astype(BF16)


def reciprocal(value):
    guess = pl.reciprocal(value, approx=True)
    for _ in range(2):
        guess = guess + guess * (1.0 - value * guess)
    return guess


def splat(tile, column):
    return jnp.broadcast_to(tile[:, column:column + 1], tile.shape)


def row_of(tile, index):
    return jnp.broadcast_to(tile[index:index + 1, :], tile.shape)


def merge_rows(tile, rows, first):
    index = lax.broadcasted_iota(jnp.int32, tile.shape, 0)
    for offset, row in enumerate(rows):
        tile = jnp.where(index == first + offset, row, tile)
    return tile


def pivot_block(tiles, step):
    block, first = step // 2, 4 * (step % 2)
    columns = [[splat(tile, 4 * step + j) for j in range(4)] for tile in tiles]
    rows = [row_of(tiles[block], first + i) for i in range(4)]
    pivots = [[row_of(columns[block][j], first + i) for j in range(4)] for i in range(4)]
    return block, first, columns, rows, pivots


def solve_spd(tiles, unknowns):
    for step in range(unknowns // 4):
        block, first, columns, rows, pivots = pivot_block(tiles, step)
        for j in range(4):
            scale = reciprocal(pivots[j][j])
            rows[j] = rows[j] * scale
            for c in range(j + 1, 4):
                pivots[j][c] = pivots[j][c] * scale
            for i in range(4):
                if i != j:
                    factor = pivots[i][j]
                    rows[i] = rows[i] - factor * rows[j]
                    for c in range(j + 1, 4):
                        pivots[i][c] = pivots[i][c] - factor * pivots[j][c]
        updated = []
        for t, tile in enumerate(tiles):
            for j in range(4):
                tile = tile - columns[t][j] * rows[j]
            if t == block:
                tile = merge_rows(tile, rows, first)
            updated.append(tile)
        tiles = updated
    return tiles


def eliminate(tiles, unknowns):
    for step in range(unknowns // 4):
        block, first, columns, rows, pivots = pivot_block(tiles, step)
        done = []
        for j in range(4):
            scale = reciprocal(pivots[j][j])
            done.append(rows[j] * lax.rsqrt(pivots[j][j]))
            rows[j] = rows[j] * scale
            for c in range(j + 1, 4):
                pivots[j][c] = pivots[j][c] * scale
            for i in range(4):
                if i != j:
                    factor = pivots[i][j]
                    rows[i] = rows[i] - factor * rows[j]
                    for c in range(j + 1, 4):
                        pivots[i][c] = pivots[i][c] - factor * pivots[j][c]
        index = lax.broadcasted_iota(jnp.int32, tiles[0].shape, 0)
        updated = []
        for t, tile in enumerate(tiles):
            if t < block:
                updated.append(tile)
                continue
            changed = tile
            for j in range(4):
                changed = changed - columns[t][j] * rows[j]
            if t == block:
                changed = jnp.where(index >= first + 4, changed, tile)
                changed = merge_rows(changed, done, first)
            updated.append(changed)
        tiles = updated
    return tiles


def all_sum(part, slots, gathered, total, sems, slabs, pencils):
    slab, pencil = lax.axis_index("slab"), lax.axis_index("pencil")
    scatter_send, scatter_recv, slab_send, slab_recv, back_send, back_recv = sems
    rows = part.shape[0] // pencils

    def chunk(index):
        return pl.ds(pl.multiple_of(index * rows, rows), rows)

    copies = []
    for d in range(1, pencils):
        peer = lax.rem(pencil + d, pencils)
        copies.append(pltpu.make_async_remote_copy(
            src_ref=part.at[chunk(peer)], dst_ref=slots.at[d - 1],
            send_sem=scatter_send.at[d - 1], recv_sem=scatter_recv.at[d - 1],
            device_id={"slab": slab, "pencil": peer}, device_id_type=MESH))
    for copy in copies:
        copy.start()
    mine = part[chunk(pencil), :]
    for d, copy in enumerate(copies):
        copy.wait_recv()
        mine = mine + slots[d]
    gathered[slab] = mine
    slab_copies = []
    for d in range(1, slabs):
        peer = lax.rem(slab + d, slabs)
        slab_copies.append(pltpu.make_async_remote_copy(
            src_ref=gathered.at[slab], dst_ref=gathered.at[slab],
            send_sem=slab_send.at[d - 1], recv_sem=slab_recv.at[d - 1],
            device_id={"slab": peer, "pencil": pencil}, device_id_type=MESH))
    for copy in slab_copies:
        copy.start()
    for copy in slab_copies:
        copy.wait_recv()
    summed = gathered[0]
    for s in range(1, slabs):
        summed = summed + gathered[s]
    total[chunk(pencil), :] = summed
    back_copies = []
    for d in range(1, pencils):
        peer = lax.rem(pencil + d, pencils)
        back_copies.append(pltpu.make_async_remote_copy(
            src_ref=total.at[chunk(pencil)], dst_ref=total.at[chunk(pencil)],
            send_sem=back_send.at[d - 1], recv_sem=back_recv.at[d - 1],
            device_id={"slab": slab, "pencil": peer}, device_id_type=MESH))
    for copy in back_copies:
        copy.start()
    for copy in back_copies:
        copy.wait_recv()
    for copy in copies + slab_copies + back_copies:
        copy.wait_send()


def gather_sum(value, slots, send, recv, axis, count):
    me = lax.axis_index(axis)
    place = {"slab": lax.axis_index("slab"), "pencil": lax.axis_index("pencil")}
    slots[me] = value
    copies = []
    for d in range(1, count):
        copies.append(pltpu.make_async_remote_copy(
            src_ref=slots.at[me], dst_ref=slots.at[me],
            send_sem=send.at[d - 1], recv_sem=recv.at[d - 1],
            device_id={**place, axis: lax.rem(me + d, count)}, device_id_type=MESH))
    for copy in copies:
        copy.start()
    for copy in copies:
        copy.wait_recv()
    total = slots[0]
    for s in range(1, count):
        total = total + slots[s]
    return total, copies


def paired(factors):
    none = jnp.zeros_like(factors)
    return jnp.concatenate([
        jnp.concatenate([factors, none], axis=1), jnp.concatenate([none, factors], axis=1)], axis=0)


def pair_product(factors, rows, keep, width):
    half = GROUP // 2
    sides = [jnp.concatenate([rows(i) for i in range(s * half, (s + 1) * half)], axis=1)
             for s in range(2)]
    if keep:
        sides = [jnp.concatenate([side, side[0:keep]], axis=0) for side in sides]
    result = jnp.dot(factors, jnp.concatenate(sides, axis=0), preferred_element_type=F32)
    count = result.shape[0] // 2
    return [result[s * count:(s + 1) * count, i * width:(i + 1) * width]
            for s in range(2) for i in range(half)]


def gram_kernel(basis_ref, image_ref, picked_ref, rows_out, sums_out, wide, gram):
    columns, height, width = basis_ref.shape
    count = picked_ref.shape[1]
    padded = rows_out.shape[1]
    low = 2 * columns - padded
    pitch = height + PITCH_EXTRA
    z = pl.program_id(0)

    @pl.when(z == 0)
    def _():
        gram[...] = jnp.zeros_like(gram)

    for which, source in enumerate((basis_ref, image_ref)):
        for c in range(columns):
            wide[pl.ds((which * columns + c) * pitch, height), :] = source[c].astype(F32)
    total = gram[...]
    for g in range(height // GROUP):
        turned_rows = []
        for y in range(g * GROUP, (g + 1) * GROUP):
            both = wide[pl.ds(y, 2 * columns, stride=pitch), :].astype(BF16)
            rows_out[y] = both[0:padded]
            turned_rows.append(both)
        stacked = jnp.concatenate(turned_rows, axis=1)
        total = total + dot_nt(stacked[low:], stacked)
    gram[...] = total

    @pl.when(z == pl.num_programs(0) - 1)
    def _():
        source_row = lax.broadcasted_iota(jnp.int32, (2 * columns, LANES), 0)
        lane = lax.broadcasted_iota(jnp.int32, (2 * columns, LANES), 1)
        column = lax.broadcasted_iota(jnp.int32, (2 * columns, count), 0)
        chosen_one = jnp.where(column == picked_ref[...], 1.0, 0.0).astype(BF16)
        place = lax.broadcasted_iota(jnp.int32, (count, LANES), 1) - columns
        place = jnp.where(
            place == lax.broadcasted_iota(jnp.int32, (count, LANES), 0), 1.0, 0.0).astype(BF16)
        select = jnp.dot(chosen_one, place, preferred_element_type=F32)
        select = jnp.where(
            jnp.logical_and(lane < columns, source_row == lane + columns), 1.0, select)
        select = select.astype(BF16)
        high, rest = total.astype(BF16), total
        augmented = jnp.dot(high, select, preferred_element_type=F32)
        for _ in range(2):
            rest = rest - high.astype(F32)
            high = rest.astype(BF16)
            augmented = augmented + jnp.dot(high, select, preferred_element_type=F32)
        sums_out[...] = augmented


def main_kernel(
    slabs, pencils, count, cells, columns,
    rows_ref, part1, material_ref,
    rec_out, app_out, inverse_out,
    rows_of_basis, weights, rec, rec_halves, app_halves, factor,
    z_send, z_halo, y_send, y_halo,
    slots1, gathered1, total1, slots2, gathered2, turned,
    in_sem, out_sems, halo_send, halo_recv, *sum_sems,
):
    depth, height, padded, width = rows_of_basis.shape
    extra = padded - columns
    groups = height // GROUP
    slab, pencil = lax.axis_index("slab"), lax.axis_index("pencil")

    load = pltpu.make_async_copy(rows_ref, rows_of_basis, in_sem)
    load.start()

    barrier = pltpu.get_barrier_semaphore()
    for d in range(1, pencils):
        pl.semaphore_signal(
            barrier, inc=1, device_id={"slab": slab, "pencil": lax.rem(pencil + d, pencils)},
            device_id_type=MESH)
    for d in range(1, slabs):
        pl.semaphore_signal(
            barrier, inc=1, device_id={"slab": lax.rem(slab + d, slabs), "pencil": pencil},
            device_id_type=MESH)

    material = material_ref[...]
    factor[...] = 6.0 - jnp.where(
        material == 0, 0.3,
        jnp.where(material == 1, 0.9, jnp.where(material == 2, 1.6, 2.5))).astype(F32)


    pl.semaphore_wait(barrier, slabs + pencils - 2)
    all_sum(part1, slots1, gathered1, total1, sum_sems[0:6], slabs, pencils)

    tiles = [total1[extra + 8 * t:extra + 8 * (t + 1), :] for t in range(columns // 8)]
    tiles = solve_spd(tiles, columns)
    turned[...] = jnp.zeros_like(turned)
    for t, tile in enumerate(tiles):
        turned[8 * t:8 * (t + 1), :] = tile
    weights[...] = paired(turned[...].T[columns:columns + count, 0:padded]).astype(BF16)
    load.wait()

    def recycle_layer(z):
        for g in range(groups):
            results = pair_product(
                weights[...], lambda i: rows_of_basis[z, g * GROUP + i], 0, width)
            for i in range(GROUP):
                rec[z + 1, 1 + g * GROUP + i] = results[i]

    def z_copy(side, peer):
        return pltpu.make_async_remote_copy(
            src_ref=z_send.at[side], dst_ref=z_halo.at[side],
            send_sem=halo_send.at[side], recv_sem=halo_recv.at[side],
            device_id={"slab": peer, "pencil": pencil}, device_id_type=MESH)

    def y_copy(side, peer):
        return pltpu.make_async_remote_copy(
            src_ref=y_send.at[side], dst_ref=y_halo.at[side],
            send_sem=halo_send.at[2 + side], recv_sem=halo_recv.at[2 + side],
            device_id={"slab": slab, "pencil": peer}, device_id_type=MESH)

    z_copies = (z_copy(0, lax.rem(slab + 1, slabs)), z_copy(1, lax.rem(slab + slabs - 1, slabs)))
    y_copies = (y_copy(0, lax.rem(pencil + 1, pencils)),
                y_copy(1, lax.rem(pencil + pencils - 1, pencils)))
    sends = (slab < slabs - 1, slab > 0, pencil < pencils - 1, pencil > 0)
    takes = (slab > 0, slab < slabs - 1, pencil > 0, pencil < pencils - 1)

    recycle_layer(depth - 1)
    z_send[0] = rec[depth, 1:height + 1].astype(BF16)
    pl.when(sends[0])(z_copies[0].start)
    recycle_layer(0)
    z_send[1] = rec[1, 1:height + 1].astype(BF16)
    pl.when(sends[1])(z_copies[1].start)
    pl.loop(1, depth - 1)(recycle_layer)
    y_send[0] = rec[1:depth + 1, height].astype(BF16)
    pl.when(sends[2])(y_copies[0].start)
    y_send[1] = rec[1:depth + 1, 1].astype(BF16)
    pl.when(sends[3])(y_copies[1].start)

    lanes = lax.broadcasted_iota(jnp.int32, (count, width), 1)

    def applied_layer(z, normal):
        for g in range(groups):
            values = []
            for y in range(g * GROUP, (g + 1) * GROUP):
                center = rec[z + 1, y + 1]
                beside = rec[z, y + 1] + rec[z + 2, y + 1] + rec[z + 1, y] + rec[z + 1, y + 2]
                beside = beside + jnp.where(lanes == 0, 0.0, pltpu.roll(center, 1, 1))
                beside = beside + jnp.where(
                    lanes == width - 1, 0.0, pltpu.roll(center, width - 1, 1))
                value = factor[z, y:y + 1, :] * center - beside
                values.append(value)
            high, rest = split(jnp.concatenate(values, axis=1))
            both = jnp.concatenate([high, rest], axis=0)
            for i in range(GROUP):
                app_halves[z, g * GROUP + i] = both[:, i * width:(i + 1) * width]
            normal = normal + dot_nt(both, both)
        return normal

    def halve_layer(z):
        for y in range(height):
            high, rest = split(rec[z + 1, y + 1])
            rec_halves[z, y] = jnp.concatenate([high, rest], axis=0)

    for side, (take, send) in enumerate(zip(takes[2:], sends[2:])):
        pl.when(take)(y_copies[side].wait_recv)

        @pl.when(jnp.logical_not(take))
        def _():
            y_halo[side] = jnp.zeros(y_halo.shape[1:], BF16)

        rec[1:depth + 1, 0 if side == 0 else height + 1] = y_halo[side].astype(F32)
    normal = lax.fori_loop(1, depth - 1, applied_layer, jnp.zeros((2 * count, 2 * count), F32))
    pl.loop(0, depth)(halve_layer)
    rec_store = pltpu.make_async_copy(rec_halves, rec_out, out_sems.at[0])
    rec_store.start()
    for side, take in enumerate(takes[:2]):
        pl.when(take)(z_copies[side].wait_recv)

        @pl.when(jnp.logical_not(take))
        def _():
            z_halo[side] = jnp.zeros(z_halo.shape[1:], BF16)

        rec[0 if side == 0 else depth + 1, 1:height + 1] = z_halo[side].astype(F32)
        normal = applied_layer(0 if side == 0 else depth - 1, normal)
    app_store = pltpu.make_async_copy(app_halves, app_out, out_sems.at[1])
    app_store.start()

    turned[0:2 * count, 0:2 * count] = normal
    halves = turned[0:count, :] + turned[count:2 * count, :]
    halves = halves + pltpu.roll(halves, LANES - count, 1)
    lane = lax.broadcasted_iota(jnp.int32, (8, LANES), 1)
    packed = halves[0:8]
    for t in range(1, count // 8):
        packed = jnp.where(
            lane < t * count, packed, pltpu.roll(halves[8 * t:8 * (t + 1)], t * count, 1))
    packed, pencil_copies = gather_sum(
        packed, slots2, sum_sems[6], sum_sems[7], "pencil", pencils)
    packed, slab_copies = gather_sum(
        packed, gathered2, sum_sems[8], sum_sems[9], "slab", slabs)
    total2 = jnp.concatenate(
        [packed] + [pltpu.roll(packed, LANES - t * count, 1) for t in range(1, count // 8)], axis=0)

    row = lax.broadcasted_iota(jnp.int32, (count, LANES), 0)
    lane = lax.broadcasted_iota(jnp.int32, (count, LANES), 1)
    matrix = jnp.where(
        lane < count, total2 * (1.0 / cells), jnp.where(lane == row + count, 1.0, 0.0))
    tiles = eliminate([matrix[8 * t:8 * (t + 1), :] for t in range(count // 8)], count)
    inverse = pltpu.roll(jnp.concatenate(tiles, axis=0), LANES - count, 1)
    inverse = jnp.where(lane <= row, inverse, 0.0)
    high = inverse.astype(BF16).astype(F32)
    rest = (inverse - high).astype(BF16).astype(F32)
    inverse_out[...] = high + pltpu.roll(high, count, 1) + pltpu.roll(rest, 2 * count, 1)

    for copy in pencil_copies + slab_copies:
        copy.wait_send()
    for copy, send in zip(z_copies + y_copies, sends):
        pl.when(send)(copy.wait_send)
    rec_store.wait()
    app_store.wait()


def final_kernel(inverse_ref, rec_ref, app_ref, rec_out, app_out, rec_wide, app_wide):
    height, count, width = rec_ref.shape[0], rec_ref.shape[1] // 2, rec_ref.shape[2]
    factors = paired(inverse_ref[...][:, 0:3 * count]).astype(BF16)
    pitch = height + PITCH_EXTRA
    for source, target, wide in ((rec_ref, rec_out, rec_wide), (app_ref, app_out, app_wide)):
        for g in range(height // GROUP):
            results = pair_product(factors, lambda i: source[g * GROUP + i], count, width)
            for i in range(GROUP):
                wide[pl.ds(g * GROUP + i, count, stride=pitch), :] = results[i]
        for k in range(count):
            target[k] = wide[pl.ds(k * pitch, height), :]


def local(slabs, pencils, basis, image, material, picked):
    columns, depth, height, width = basis.shape
    count = picked.shape[0]
    extra = 16 - columns % 16 if columns % 16 else 0
    padded = columns + extra
    cells = depth * height * width * slabs * pencils

    def sum_scratch(rows):
        return [
            pltpu.VMEM((pencils - 1, rows // pencils, LANES), F32),
            pltpu.VMEM((slabs, rows // pencils, LANES), F32),
            pltpu.VMEM((rows, LANES), F32),
        ]

    def sum_sems(*counts):
        return [pltpu.SemaphoreType.DMA((n - 1,)) for n in counts]

    in_vmem = pl.BlockSpec(memory_space=pltpu.VMEM)
    anywhere = pl.BlockSpec(memory_space=pl.ANY)
    turned_shape = jax.ShapeDtypeStruct((depth, height, 2 * count, width), BF16)
    column_block = pl.BlockSpec((columns, None, height, width), lambda z: (0, z, 0, 0))
    rows, sums = pl.pallas_call(
        gram_kernel,
        grid=(depth,),
        out_shape=(jax.ShapeDtypeStruct((depth, height, padded, width), BF16),
                   jax.ShapeDtypeStruct((padded, LANES), F32)),
        in_specs=[column_block, column_block, pl.BlockSpec((1, count), lambda z: (0, 0))],
        out_specs=(pl.BlockSpec((None, height, padded, width), lambda z: (z, 0, 0, 0)),
                   pl.BlockSpec((padded, LANES), lambda z: (0, 0))),
        scratch_shapes=[
            pltpu.VMEM((2 * columns * (height + PITCH_EXTRA), width), F32),
            pltpu.VMEM((padded, 2 * columns), F32),
        ],
        compiler_params=pltpu.CompilerParams(vmem_limit_bytes=60 * 1024 * 1024),
        name="gram_matrices",
    )(basis, image, picked[None, :])
    rec, app, inverse = pl.pallas_call(
        functools.partial(main_kernel, slabs, pencils, count, cells, columns),
        out_shape=(turned_shape, turned_shape, jax.ShapeDtypeStruct((count, LANES), F32)),
        in_specs=[anywhere, in_vmem, in_vmem],
        out_specs=(anywhere, anywhere, in_vmem),
        scratch_shapes=[
            pltpu.VMEM((depth, height, padded, width), BF16),
            pltpu.VMEM((2 * count, 2 * padded), BF16),
            pltpu.VMEM((depth + 2, height + 2, count, width), F32),
            pltpu.VMEM((depth, height, 2 * count, width), BF16),
            pltpu.VMEM((depth, height, 2 * count, width), BF16),
            pltpu.VMEM((depth, height, width), F32),
            pltpu.VMEM((2, height, count, width), BF16),
            pltpu.VMEM((2, height, count, width), BF16),
            pltpu.VMEM((2, depth, count, width), BF16),
            pltpu.VMEM((2, depth, count, width), BF16),
            *sum_scratch(padded),
            pltpu.VMEM((pencils, 8, LANES), F32),
            pltpu.VMEM((slabs, 8, LANES), F32),
            pltpu.VMEM((LANES, LANES), F32),
            pltpu.SemaphoreType.DMA(()),
            pltpu.SemaphoreType.DMA((2,)),
            pltpu.SemaphoreType.DMA((4,)),
            pltpu.SemaphoreType.DMA((4,)),
            *sum_sems(pencils, pencils, slabs, slabs, pencils, pencils),
            *sum_sems(pencils, pencils, slabs, slabs),
        ],
        compiler_params=pltpu.CompilerParams(
            collective_id=0, has_side_effects=True, vmem_limit_bytes=60 * 1024 * 1024),
        name="recycle_update",
    )(rows, sums, material)
    whole = pl.BlockSpec((None, height, 2 * count, width), lambda z: (z, 0, 0, 0))
    placed = pl.BlockSpec((count, None, height, width), lambda z: (0, z, 0, 0))
    out = jax.ShapeDtypeStruct((count, depth, height, width), F32)
    return pl.pallas_call(
        final_kernel,
        grid=(depth,),
        out_shape=(out, out),
        in_specs=[pl.BlockSpec((count, LANES), lambda z: (0, 0)), whole, whole],
        out_specs=(placed, placed),
        scratch_shapes=[pltpu.VMEM((count * (height + PITCH_EXTRA), width), F32)] * 2,
        compiler_params=pltpu.CompilerParams(vmem_limit_bytes=60 * 1024 * 1024),
        name="times_inverse",
    )(inverse, rec, app)


def solution(mesh):
    placed = (
        P(None, "slab", "pencil", None),
        P(None, "slab", "pencil", None),
        P("slab", "pencil", None),
        P(),
    )
    return jax.shard_map(
        functools.partial(local, mesh.shape["slab"], mesh.shape["pencil"]),
        mesh=mesh,
        in_specs=placed,
        out_specs=(P(None, "slab", "pencil", None), P(None, "slab", "pencil", None)),
        check_vma=False,
    )
```

```python
import functools

import jax
import jax.numpy as jnp
from jax import lax
from jax.experimental import pallas as pl
from jax.experimental.pallas import tpu as pltpu
from jax.sharding import PartitionSpec as P

MESH = pl.DeviceIdType.MESH
F32 = jnp.float32
BF16 = jnp.bfloat16
GROUP = 8
PITCH_EXTRA = 1
LANES = 128


def dot_nt(a, b):
    return lax.dot_general(a, b, (((1,), (1,)), ((), ())), preferred_element_type=F32)


def split(value):
    high = value.astype(BF16)
    return high, (value - high.astype(F32)).astype(BF16)


def reciprocal(value):
    guess = pl.reciprocal(value, approx=True)
    for _ in range(2):
        guess = guess + guess * (1.0 - value * guess)
    return guess


def splat(tile, column):
    return jnp.broadcast_to(tile[:, column:column + 1], tile.shape)


def row_of(tile, index):
    return jnp.broadcast_to(tile[index:index + 1, :], tile.shape)


def merge_rows(tile, rows, first):
    index = lax.broadcasted_iota(jnp.int32, tile.shape, 0)
    for offset, row in enumerate(rows):
        tile = jnp.where(index == first + offset, row, tile)
    return tile


def pivot_block(tiles, step):
    block, first = step // 2, 4 * (step % 2)
    columns = [[splat(tile, 4 * step + j) for j in range(4)] for tile in tiles]
    rows = [row_of(tiles[block], first + i) for i in range(4)]
    pivots = [[row_of(columns[block][j], first + i) for j in range(4)] for i in range(4)]
    return block, first, columns, rows, pivots


def solve_spd(tiles, unknowns):
    for step in range(unknowns // 4):
        block, first, columns, rows, pivots = pivot_block(tiles, step)
        for j in range(4):
            scale = reciprocal(pivots[j][j])
            rows[j] = rows[j] * scale
            for c in range(j + 1, 4):
                pivots[j][c] = pivots[j][c] * scale
            for i in range(4):
                if i != j:
                    factor = pivots[i][j]
                    rows[i] = rows[i] - factor * rows[j]
                    for c in range(j + 1, 4):
                        pivots[i][c] = pivots[i][c] - factor * pivots[j][c]
        updated = []
        for t, tile in enumerate(tiles):
            for j in range(4):
                tile = tile - columns[t][j] * rows[j]
            if t == block:
                tile = merge_rows(tile, rows, first)
            updated.append(tile)
        tiles = updated
    return tiles


def eliminate(tiles, unknowns):
    for step in range(unknowns // 4):
        block, first, columns, rows, pivots = pivot_block(tiles, step)
        done = []
        for j in range(4):
            scale = reciprocal(pivots[j][j])
            done.append(rows[j] * lax.rsqrt(pivots[j][j]))
            rows[j] = rows[j] * scale
            for c in range(j + 1, 4):
                pivots[j][c] = pivots[j][c] * scale
            for i in range(4):
                if i != j:
                    factor = pivots[i][j]
                    rows[i] = rows[i] - factor * rows[j]
                    for c in range(j + 1, 4):
                        pivots[i][c] = pivots[i][c] - factor * pivots[j][c]
        index = lax.broadcasted_iota(jnp.int32, tiles[0].shape, 0)
        updated = []
        for t, tile in enumerate(tiles):
            if t < block:
                updated.append(tile)
                continue
            changed = tile
            for j in range(4):
                changed = changed - columns[t][j] * rows[j]
            if t == block:
                changed = jnp.where(index >= first + 4, changed, tile)
                changed = merge_rows(changed, done, first)
            updated.append(changed)
        tiles = updated
    return tiles


def all_sum(part, slots, gathered, total, sems, slabs, pencils):
    slab, pencil = lax.axis_index("slab"), lax.axis_index("pencil")
    scatter_send, scatter_recv, slab_send, slab_recv, back_send, back_recv = sems
    rows = part.shape[0] // pencils

    def chunk(index):
        return pl.ds(pl.multiple_of(index * rows, rows), rows)

    copies = []
    for d in range(1, pencils):
        peer = lax.rem(pencil + d, pencils)
        copies.append(pltpu.make_async_remote_copy(
            src_ref=part.at[chunk(peer)], dst_ref=slots.at[d - 1],
            send_sem=scatter_send.at[d - 1], recv_sem=scatter_recv.at[d - 1],
            device_id={"slab": slab, "pencil": peer}, device_id_type=MESH))
    for copy in copies:
        copy.start()
    mine = part[chunk(pencil), :]
    for d, copy in enumerate(copies):
        copy.wait_recv()
        mine = mine + slots[d]
    gathered[slab] = mine
    slab_copies = []
    for d in range(1, slabs):
        peer = lax.rem(slab + d, slabs)
        slab_copies.append(pltpu.make_async_remote_copy(
            src_ref=gathered.at[slab], dst_ref=gathered.at[slab],
            send_sem=slab_send.at[d - 1], recv_sem=slab_recv.at[d - 1],
            device_id={"slab": peer, "pencil": pencil}, device_id_type=MESH))
    for copy in slab_copies:
        copy.start()
    for copy in slab_copies:
        copy.wait_recv()
    summed = gathered[0]
    for s in range(1, slabs):
        summed = summed + gathered[s]
    total[chunk(pencil), :] = summed
    back_copies = []
    for d in range(1, pencils):
        peer = lax.rem(pencil + d, pencils)
        back_copies.append(pltpu.make_async_remote_copy(
            src_ref=total.at[chunk(pencil)], dst_ref=total.at[chunk(pencil)],
            send_sem=back_send.at[d - 1], recv_sem=back_recv.at[d - 1],
            device_id={"slab": slab, "pencil": peer}, device_id_type=MESH))
    for copy in back_copies:
        copy.start()
    for copy in back_copies:
        copy.wait_recv()
    for copy in copies + slab_copies + back_copies:
        copy.wait_send()


def gather_sum(value, slots, send, recv, axis, count):
    me = lax.axis_index(axis)
    place = {"slab": lax.axis_index("slab"), "pencil": lax.axis_index("pencil")}
    slots[me] = value
    copies = []
    for d in range(1, count):
        copies.append(pltpu.make_async_remote_copy(
            src_ref=slots.at[me], dst_ref=slots.at[me],
            send_sem=send.at[d - 1], recv_sem=recv.at[d - 1],
            device_id={**place, axis: lax.rem(me + d, count)}, device_id_type=MESH))
    for copy in copies:
        copy.start()
    for copy in copies:
        copy.wait_recv()
    total = slots[0]
    for s in range(1, count):
        total = total + slots[s]
    return total, copies


def paired(factors):
    none = jnp.zeros_like(factors)
    return jnp.concatenate([
        jnp.concatenate([factors, none], axis=1), jnp.concatenate([none, factors], axis=1)], axis=0)


def pair_product(factors, rows, keep, width):
    half = GROUP // 2
    sides = [jnp.concatenate([rows(i) for i in range(s * half, (s + 1) * half)], axis=1)
             for s in range(2)]
    if keep:
        sides = [jnp.concatenate([side, side[0:keep]], axis=0) for side in sides]
    result = jnp.dot(factors, jnp.concatenate(sides, axis=0), preferred_element_type=F32)
    count = result.shape[0] // 2
    return [result[s * count:(s + 1) * count, i * width:(i + 1) * width]
            for s in range(2) for i in range(half)]


def main_kernel(
    slabs, pencils, count, cells,
    basis_ref, image_ref, material_ref, picked_ref,
    rec_out, app_out, inverse_out,
    basis_in, image_in, wide, rows_of_basis, weights, rec, rec_halves, app_halves, factor,
    z_send, z_halo, y_send, y_halo,
    part1, slots1, gathered1, total1, slots2, gathered2, turned,
    in_sems, out_sems, halo_send, halo_recv, *sum_sems,
):
    columns, depth, height, width = basis_in.shape[1], *basis_in.shape[:1], *basis_in.shape[2:]
    groups = height // GROUP
    slab, pencil = lax.axis_index("slab"), lax.axis_index("pencil")

    loads = []
    for z in range(depth):
        for which, (source, target) in enumerate(((basis_ref, basis_in), (image_ref, image_in))):
            loads.append(pltpu.make_async_copy(
                source.at[:, z], target.at[z], in_sems.at[2 * z + which]))
    for load in loads:
        load.start()

    barrier = pltpu.get_barrier_semaphore()
    for d in range(1, pencils):
        pl.semaphore_signal(
            barrier, inc=1, device_id={"slab": slab, "pencil": lax.rem(pencil + d, pencils)},
            device_id_type=MESH)
    for d in range(1, slabs):
        pl.semaphore_signal(
            barrier, inc=1, device_id={"slab": lax.rem(slab + d, slabs), "pencil": pencil},
            device_id_type=MESH)

    material = material_ref[...]
    factor[...] = 6.0 - jnp.where(
        material == 0, 0.3,
        jnp.where(material == 1, 0.9, jnp.where(material == 2, 1.6, 2.5))).astype(F32)

    extra = 16 - columns % 16 if columns % 16 else 0
    low = columns - extra
    pitch = height + PITCH_EXTRA

    def gram_layer(z, gram):
        for which, (source, target) in enumerate(((basis_ref, basis_in), (image_ref, image_in))):
            pltpu.make_async_copy(
                source.at[:, z], target.at[z], in_sems.at[2 * z + which]).wait()
            for c in range(columns):
                wide[pl.ds((which * columns + c) * pitch, height), :] = target[z, c].astype(F32)
        for g in range(groups):
            turned_rows = []
            for y in range(g * GROUP, (g + 1) * GROUP):
                both = wide[pl.ds(y, 2 * columns, stride=pitch), :].astype(BF16)
                rows_of_basis[z, y] = both[0:columns + extra]
                turned_rows.append(both)
            stacked = jnp.concatenate(turned_rows, axis=1)
            gram = gram + dot_nt(stacked[low:], stacked)
        return gram

    gram = lax.fori_loop(
        0, depth, gram_layer, jnp.zeros((columns + extra, 2 * columns), F32))

    source_row = lax.broadcasted_iota(jnp.int32, (2 * columns, LANES), 0)
    lane = lax.broadcasted_iota(jnp.int32, (2 * columns, LANES), 1)
    column = lax.broadcasted_iota(jnp.int32, (2 * columns, count), 0)
    chosen_one = jnp.where(column == picked_ref[...], 1.0, 0.0).astype(BF16)
    place = lax.broadcasted_iota(jnp.int32, (count, LANES), 1) - columns
    place = jnp.where(
        place == lax.broadcasted_iota(jnp.int32, (count, LANES), 0), 1.0, 0.0).astype(BF16)
    select = jnp.dot(chosen_one, place, preferred_element_type=F32)
    select = jnp.where(
        jnp.logical_and(lane < columns, source_row == lane + columns), 1.0, select).astype(BF16)
    high, rest = gram.astype(BF16), gram
    augmented = jnp.dot(high, select, preferred_element_type=F32)
    for _ in range(2):
        rest = rest - high.astype(F32)
        high = rest.astype(BF16)
        augmented = augmented + jnp.dot(high, select, preferred_element_type=F32)
    part1[...] = augmented

    pl.semaphore_wait(barrier, slabs + pencils - 2)
    all_sum(part1, slots1, gathered1, total1, sum_sems[0:6], slabs, pencils)

    tiles = [total1[extra + 8 * t:extra + 8 * (t + 1), :] for t in range(columns // 8)]
    tiles = solve_spd(tiles, columns)
    turned[...] = jnp.zeros_like(turned)
    for t, tile in enumerate(tiles):
        turned[8 * t:8 * (t + 1), :] = tile
    weights[...] = paired(
        turned[...].T[columns:columns + count, 0:columns + extra]).astype(BF16)

    def recycle_layer(z):
        for g in range(groups):
            results = pair_product(
                weights[...], lambda i: rows_of_basis[z, g * GROUP + i], 0, width)
            for i in range(GROUP):
                rec[z + 1, 1 + g * GROUP + i] = results[i]

    def z_copy(side, peer):
        return pltpu.make_async_remote_copy(
            src_ref=z_send.at[side], dst_ref=z_halo.at[side],
            send_sem=halo_send.at[side], recv_sem=halo_recv.at[side],
            device_id={"slab": peer, "pencil": pencil}, device_id_type=MESH)

    def y_copy(side, peer):
        return pltpu.make_async_remote_copy(
            src_ref=y_send.at[side], dst_ref=y_halo.at[side],
            send_sem=halo_send.at[2 + side], recv_sem=halo_recv.at[2 + side],
            device_id={"slab": slab, "pencil": peer}, device_id_type=MESH)

    z_copies = (z_copy(0, lax.rem(slab + 1, slabs)), z_copy(1, lax.rem(slab + slabs - 1, slabs)))
    y_copies = (y_copy(0, lax.rem(pencil + 1, pencils)),
                y_copy(1, lax.rem(pencil + pencils - 1, pencils)))
    sends = (slab < slabs - 1, slab > 0, pencil < pencils - 1, pencil > 0)
    takes = (slab > 0, slab < slabs - 1, pencil > 0, pencil < pencils - 1)

    for side, y in enumerate((height - 1, 0)):
        for first in range(0, depth, GROUP):
            edge = pair_product(weights[...], lambda i: rows_of_basis[first + i, y], 0, width)
            for i in range(GROUP):
                y_send[side, first + i] = edge[i].astype(BF16)
        pl.when(sends[2 + side])(y_copies[side].start)
    recycle_layer(depth - 1)
    z_send[0] = rec[depth, 1:height + 1].astype(BF16)
    pl.when(sends[0])(z_copies[0].start)
    recycle_layer(0)
    z_send[1] = rec[1, 1:height + 1].astype(BF16)
    pl.when(sends[1])(z_copies[1].start)
    pl.loop(1, depth - 1)(recycle_layer)

    lanes = lax.broadcasted_iota(jnp.int32, (count, width), 1)

    def applied_layer(z, normal):
        for g in range(groups):
            values = []
            for y in range(g * GROUP, (g + 1) * GROUP):
                center = rec[z + 1, y + 1]
                beside = rec[z, y + 1] + rec[z + 2, y + 1] + rec[z + 1, y] + rec[z + 1, y + 2]
                beside = beside + jnp.where(lanes == 0, 0.0, pltpu.roll(center, 1, 1))
                beside = beside + jnp.where(
                    lanes == width - 1, 0.0, pltpu.roll(center, width - 1, 1))
                value = factor[z, y:y + 1, :] * center - beside
                values.append(value)
            high, rest = split(jnp.concatenate(values, axis=1))
            both = jnp.concatenate([high, rest], axis=0)
            for i in range(GROUP):
                app_halves[z, g * GROUP + i] = both[:, i * width:(i + 1) * width]
            normal = normal + dot_nt(both, both)
        return normal

    def halve_layer(z):
        for y in range(height):
            high, rest = split(rec[z + 1, y + 1])
            rec_halves[z, y] = jnp.concatenate([high, rest], axis=0)

    pl.loop(0, depth)(halve_layer)
    rec_store = pltpu.make_async_copy(rec_halves, rec_out, out_sems.at[0])
    rec_store.start()
    for side, take in enumerate(takes[2:]):
        pl.when(take)(y_copies[side].wait_recv)

        @pl.when(jnp.logical_not(take))
        def _():
            y_halo[side] = jnp.zeros(y_halo.shape[1:], BF16)

        rec[1:depth + 1, 0 if side == 0 else height + 1] = y_halo[side].astype(F32)
    normal = lax.fori_loop(1, depth - 1, applied_layer, jnp.zeros((2 * count, 2 * count), F32))
    for side, take in enumerate(takes[:2]):
        pl.when(take)(z_copies[side].wait_recv)

        @pl.when(jnp.logical_not(take))
        def _():
            z_halo[side] = jnp.zeros(z_halo.shape[1:], BF16)

        rec[0 if side == 0 else depth + 1, 1:height + 1] = z_halo[side].astype(F32)
        normal = applied_layer(0 if side == 0 else depth - 1, normal)
    app_store = pltpu.make_async_copy(app_halves, app_out, out_sems.at[1])
    app_store.start()

    turned[0:2 * count, 0:2 * count] = normal
    halves = turned[0:count, :] + turned[count:2 * count, :]
    halves = halves + pltpu.roll(halves, LANES - count, 1)
    lane = lax.broadcasted_iota(jnp.int32, (8, LANES), 1)
    packed = halves[0:8]
    for t in range(1, count // 8):
        packed = jnp.where(
            lane < t * count, packed, pltpu.roll(halves[8 * t:8 * (t + 1)], t * count, 1))
    packed, pencil_copies = gather_sum(
        packed, slots2, sum_sems[6], sum_sems[7], "pencil", pencils)
    packed, slab_copies = gather_sum(
        packed, gathered2, sum_sems[8], sum_sems[9], "slab", slabs)
    total2 = jnp.concatenate(
        [packed] + [pltpu.roll(packed, LANES - t * count, 1) for t in range(1, count // 8)], axis=0)

    row = lax.broadcasted_iota(jnp.int32, (count, LANES), 0)
    lane = lax.broadcasted_iota(jnp.int32, (count, LANES), 1)
    matrix = jnp.where(
        lane < count, total2 * (1.0 / cells), jnp.where(lane == row + count, 1.0, 0.0))
    tiles = eliminate([matrix[8 * t:8 * (t + 1), :] for t in range(count // 8)], count)
    inverse = pltpu.roll(jnp.concatenate(tiles, axis=0), LANES - count, 1)
    inverse = jnp.where(lane <= row, inverse, 0.0)
    high = inverse.astype(BF16).astype(F32)
    rest = (inverse - high).astype(BF16).astype(F32)
    inverse_out[...] = high + pltpu.roll(high, count, 1) + pltpu.roll(rest, 2 * count, 1)

    for copy in pencil_copies + slab_copies:
        copy.wait_send()
    for copy, send in zip(z_copies + y_copies, sends):
        pl.when(send)(copy.wait_send)
    rec_store.wait()
    app_store.wait()


def final_kernel(inverse_ref, rec_ref, app_ref, rec_out, app_out, rec_wide, app_wide):
    height, count, width = rec_ref.shape[0], rec_ref.shape[1] // 2, rec_ref.shape[2]
    factors = paired(inverse_ref[...][:, 0:3 * count]).astype(BF16)
    pitch = height + PITCH_EXTRA
    for source, target, wide in ((rec_ref, rec_out, rec_wide), (app_ref, app_out, app_wide)):
        for g in range(height // GROUP):
            results = pair_product(factors, lambda i: source[g * GROUP + i], count, width)
            for i in range(GROUP):
                wide[pl.ds(g * GROUP + i, count, stride=pitch), :] = results[i]
        for k in range(count):
            target[k] = wide[pl.ds(k * pitch, height), :]


def local(slabs, pencils, basis, image, material, picked):
    columns, depth, height, width = basis.shape
    count = picked.shape[0]
    extra = 16 - columns % 16 if columns % 16 else 0
    padded = columns + extra
    cells = depth * height * width * slabs * pencils

    def sum_scratch(rows):
        return [
            pltpu.VMEM((rows, LANES), F32),
            pltpu.VMEM((pencils - 1, rows // pencils, LANES), F32),
            pltpu.VMEM((slabs, rows // pencils, LANES), F32),
            pltpu.VMEM((rows, LANES), F32),
        ]

    def sum_sems(*counts):
        return [pltpu.SemaphoreType.DMA((n - 1,)) for n in counts]

    in_vmem = pl.BlockSpec(memory_space=pltpu.VMEM)
    anywhere = pl.BlockSpec(memory_space=pl.ANY)
    turned_shape = jax.ShapeDtypeStruct((depth, height, 2 * count, width), BF16)
    rec, app, inverse = pl.pallas_call(
        functools.partial(main_kernel, slabs, pencils, count, cells),
        out_shape=(turned_shape, turned_shape, jax.ShapeDtypeStruct((count, LANES), F32)),
        in_specs=[anywhere, anywhere, in_vmem, in_vmem],
        out_specs=(anywhere, anywhere, in_vmem),
        scratch_shapes=[
            pltpu.VMEM((depth, columns, height, width), BF16),
            pltpu.VMEM((depth, columns, height, width), BF16),
            pltpu.VMEM((2 * columns * (height + PITCH_EXTRA), width), F32),
            pltpu.VMEM((depth, height, padded, width), BF16),
            pltpu.VMEM((2 * count, 2 * padded), BF16),
            pltpu.VMEM((depth + 2, height + 2, count, width), F32),
            pltpu.VMEM((depth, height, 2 * count, width), BF16),
            pltpu.VMEM((depth, height, 2 * count, width), BF16),
            pltpu.VMEM((depth, height, width), F32),
            pltpu.VMEM((2, height, count, width), BF16),
            pltpu.VMEM((2, height, count, width), BF16),
            pltpu.VMEM((2, depth, count, width), BF16),
            pltpu.VMEM((2, depth, count, width), BF16),
            *sum_scratch(padded),
            pltpu.VMEM((pencils, 8, LANES), F32),
            pltpu.VMEM((slabs, 8, LANES), F32),
            pltpu.VMEM((LANES, LANES), F32),
            pltpu.SemaphoreType.DMA((2 * depth,)),
            pltpu.SemaphoreType.DMA((2,)),
            pltpu.SemaphoreType.DMA((4,)),
            pltpu.SemaphoreType.DMA((4,)),
            *sum_sems(pencils, pencils, slabs, slabs, pencils, pencils),
            *sum_sems(pencils, pencils, slabs, slabs),
        ],
        compiler_params=pltpu.CompilerParams(
            collective_id=0, has_side_effects=True, vmem_limit_bytes=56 * 1024 * 1024),
        name="recycle_update",
    )(basis, image, material, picked[None, :])
    whole = pl.BlockSpec((None, height, 2 * count, width), lambda z: (z, 0, 0, 0))
    placed = pl.BlockSpec((count, None, height, width), lambda z: (0, z, 0, 0))
    out = jax.ShapeDtypeStruct((count, depth, height, width), F32)
    return pl.pallas_call(
        final_kernel,
        grid=(depth,),
        out_shape=(out, out),
        in_specs=[pl.BlockSpec((count, LANES), lambda z: (0, 0)), whole, whole],
        out_specs=(placed, placed),
        scratch_shapes=[pltpu.VMEM((count * (height + PITCH_EXTRA), width), F32)] * 2,
        compiler_params=pltpu.CompilerParams(vmem_limit_bytes=60 * 1024 * 1024),
        name="times_inverse",
    )(inverse, rec, app)


def solution(mesh):
    placed = (
        P(None, "slab", "pencil", None),
        P(None, "slab", "pencil", None),
        P("slab", "pencil", None),
        P(),
    )
    return jax.shard_map(
        functools.partial(local, mesh.shape["slab"], mesh.shape["pencil"]),
        mesh=mesh,
        in_specs=placed,
        out_specs=(P(None, "slab", "pencil", None), P(None, "slab", "pencil", None)),
        check_vma=False,
    )
```

```python
import functools

import jax
import jax.numpy as jnp
from jax import lax
from jax.experimental import pallas as pl
from jax.experimental.pallas import tpu as pltpu
from jax.sharding import PartitionSpec as P

MESH = pl.DeviceIdType.MESH
F32 = jnp.float32
BF16 = jnp.bfloat16
GROUP = 8
PITCH_EXTRA = 1
LANES = 128
PIVOTS = 8


def dot_nt(a, b):
    return lax.dot_general(a, b, (((1,), (1,)), ((), ())), preferred_element_type=F32)


def split(value):
    high = value.astype(BF16)
    return high, (value - high.astype(F32)).astype(BF16)


def reciprocal(value):
    guess = pl.reciprocal(value, approx=True)
    for _ in range(2):
        guess = guess + guess * (1.0 - value * guess)
    return guess


def splat(tile, column):
    return jnp.broadcast_to(tile[:, column:column + 1], tile.shape)


def row_of(tile, index):
    return jnp.broadcast_to(tile[index:index + 1, :], tile.shape)


def merge_rows(tile, rows):
    index = lax.broadcasted_iota(jnp.int32, tile.shape, 0)
    for offset, row in enumerate(rows):
        tile = jnp.where(index == offset, row, tile)
    return tile


def pivot_block(tiles, step):
    columns = [[splat(tile, PIVOTS * step + j) for j in range(PIVOTS)] for tile in tiles]
    rows = [row_of(tiles[step], i) for i in range(PIVOTS)]
    pivots = [[row_of(columns[step][j], i) for j in range(PIVOTS)] for i in range(PIVOTS)]
    return columns, rows, pivots


def solve_spd(tiles, unknowns):
    for step in range(unknowns // PIVOTS):
        columns, rows, pivots = pivot_block(tiles, step)
        for j in range(PIVOTS):
            scale = reciprocal(pivots[j][j])
            rows[j] = rows[j] * scale
            for c in range(j + 1, PIVOTS):
                pivots[j][c] = pivots[j][c] * scale
            for i in range(PIVOTS):
                if i != j:
                    factor = pivots[i][j]
                    rows[i] = rows[i] - factor * rows[j]
                    for c in range(j + 1, PIVOTS):
                        pivots[i][c] = pivots[i][c] - factor * pivots[j][c]
        updated = []
        for t, tile in enumerate(tiles):
            for j in range(PIVOTS):
                tile = tile - columns[t][j] * rows[j]
            updated.append(merge_rows(tile, rows) if t == step else tile)
        tiles = updated
    return tiles


def eliminate(tiles, unknowns):
    for step in range(unknowns // PIVOTS):
        columns, rows, pivots = pivot_block(tiles, step)
        done = []
        for j in range(PIVOTS):
            scale = reciprocal(pivots[j][j])
            done.append(rows[j] * lax.rsqrt(pivots[j][j]))
            rows[j] = rows[j] * scale
            for c in range(j + 1, PIVOTS):
                pivots[j][c] = pivots[j][c] * scale
            for i in range(PIVOTS):
                if i != j:
                    factor = pivots[i][j]
                    rows[i] = rows[i] - factor * rows[j]
                    for c in range(j + 1, PIVOTS):
                        pivots[i][c] = pivots[i][c] - factor * pivots[j][c]
        updated = []
        for t, tile in enumerate(tiles):
            if t == step:
                tile = merge_rows(tile, done)
            elif t > step:
                for j in range(PIVOTS):
                    tile = tile - columns[t][j] * rows[j]
            updated.append(tile)
        tiles = updated
    return tiles


def all_sum(part, slots, gathered, total, sems, slabs, pencils):
    slab, pencil = lax.axis_index("slab"), lax.axis_index("pencil")
    scatter_send, scatter_recv, slab_send, slab_recv, back_send, back_recv = sems
    rows = part.shape[0] // pencils

    def chunk(index):
        return pl.ds(pl.multiple_of(index * rows, rows), rows)

    copies = []
    for d in range(1, pencils):
        peer = lax.rem(pencil + d, pencils)
        copies.append(pltpu.make_async_remote_copy(
            src_ref=part.at[chunk(peer)], dst_ref=slots.at[d - 1],
            send_sem=scatter_send.at[d - 1], recv_sem=scatter_recv.at[d - 1],
            device_id={"slab": slab, "pencil": peer}, device_id_type=MESH))
    for copy in copies:
        copy.start()
    mine = part[chunk(pencil), :]
    for d, copy in enumerate(copies):
        copy.wait_recv()
        mine = mine + slots[d]
    gathered[slab] = mine
    slab_copies = []
    for d in range(1, slabs):
        peer = lax.rem(slab + d, slabs)
        slab_copies.append(pltpu.make_async_remote_copy(
            src_ref=gathered.at[slab], dst_ref=gathered.at[slab],
            send_sem=slab_send.at[d - 1], recv_sem=slab_recv.at[d - 1],
            device_id={"slab": peer, "pencil": pencil}, device_id_type=MESH))
    for copy in slab_copies:
        copy.start()
    for copy in slab_copies:
        copy.wait_recv()
    summed = gathered[0]
    for s in range(1, slabs):
        summed = summed + gathered[s]
    total[chunk(pencil), :] = summed
    back_copies = []
    for d in range(1, pencils):
        peer = lax.rem(pencil + d, pencils)
        back_copies.append(pltpu.make_async_remote_copy(
            src_ref=total.at[chunk(pencil)], dst_ref=total.at[chunk(pencil)],
            send_sem=back_send.at[d - 1], recv_sem=back_recv.at[d - 1],
            device_id={"slab": slab, "pencil": peer}, device_id_type=MESH))
    for copy in back_copies:
        copy.start()
    for copy in back_copies:
        copy.wait_recv()
    for copy in copies + slab_copies + back_copies:
        copy.wait_send()


def gather_sum(value, slots, send, recv, axis, count):
    me = lax.axis_index(axis)
    place = {"slab": lax.axis_index("slab"), "pencil": lax.axis_index("pencil")}
    slots[me] = value
    copies = []
    for d in range(1, count):
        copies.append(pltpu.make_async_remote_copy(
            src_ref=slots.at[me], dst_ref=slots.at[me],
            send_sem=send.at[d - 1], recv_sem=recv.at[d - 1],
            device_id={**place, axis: lax.rem(me + d, count)}, device_id_type=MESH))
    for copy in copies:
        copy.start()
    for copy in copies:
        copy.wait_recv()
    total = slots[0]
    for s in range(1, count):
        total = total + slots[s]
    return total, copies


def paired(factors):
    none = jnp.zeros_like(factors)
    return jnp.concatenate([
        jnp.concatenate([factors, none], axis=1), jnp.concatenate([none, factors], axis=1)], axis=0)


def pair_product(factors, rows, keep, width):
    half = GROUP // 2
    sides = [jnp.concatenate([rows(i) for i in range(s * half, (s + 1) * half)], axis=1)
             for s in range(2)]
    if keep:
        sides = [jnp.concatenate([side, side[0:keep]], axis=0) for side in sides]
    result = jnp.dot(factors, jnp.concatenate(sides, axis=0), preferred_element_type=F32)
    count = result.shape[0] // 2
    return [result[s * count:(s + 1) * count, i * width:(i + 1) * width]
            for s in range(2) for i in range(half)]


def main_kernel(
    slabs, pencils, count, cells,
    basis_ref, image_ref, material_ref, picked_ref,
    rec_out, app_out, inverse_out,
    basis_in, image_in, wide, rows_of_basis, weights, rec, rec_halves, app_halves, factor,
    z_send, z_halo, y_send, y_halo,
    part1, slots1, gathered1, total1, slots2, gathered2, turned,
    in_sems, out_sems, halo_send, halo_recv, *sum_sems,
):
    columns, depth, height, width = basis_in.shape[1], *basis_in.shape[:1], *basis_in.shape[2:]
    groups = height // GROUP
    slab, pencil = lax.axis_index("slab"), lax.axis_index("pencil")

    loads = []
    for z in range(depth):
        for which, (source, target) in enumerate(((basis_ref, basis_in), (image_ref, image_in))):
            loads.append(pltpu.make_async_copy(
                source.at[:, z], target.at[z], in_sems.at[2 * z + which]))
    for load in loads:
        load.start()

    barrier = pltpu.get_barrier_semaphore()
    for d in range(1, pencils):
        pl.semaphore_signal(
            barrier, inc=1, device_id={"slab": slab, "pencil": lax.rem(pencil + d, pencils)},
            device_id_type=MESH)
    for d in range(1, slabs):
        pl.semaphore_signal(
            barrier, inc=1, device_id={"slab": lax.rem(slab + d, slabs), "pencil": pencil},
            device_id_type=MESH)

    material = material_ref[...]
    factor[...] = 6.0 - jnp.where(
        material == 0, 0.3,
        jnp.where(material == 1, 0.9, jnp.where(material == 2, 1.6, 2.5))).astype(F32)

    extra = 16 - columns % 16 if columns % 16 else 0
    low = columns - extra
    pitch = height + PITCH_EXTRA

    def gram_layer(z, gram):
        for which, (source, target) in enumerate(((basis_ref, basis_in), (image_ref, image_in))):
            pltpu.make_async_copy(
                source.at[:, z], target.at[z], in_sems.at[2 * z + which]).wait()
            for c in range(columns):
                wide[pl.ds((which * columns + c) * pitch, height), :] = target[z, c].astype(F32)
        for g in range(groups):
            turned_rows = []
            for y in range(g * GROUP, (g + 1) * GROUP):
                both = wide[pl.ds(y, 2 * columns, stride=pitch), :].astype(BF16)
                rows_of_basis[z, y] = both[0:columns + extra]
                turned_rows.append(both)
            stacked = jnp.concatenate(turned_rows, axis=1)
            gram = gram + dot_nt(stacked[low:], stacked)
        return gram

    gram = lax.fori_loop(
        0, depth, gram_layer, jnp.zeros((columns + extra, 2 * columns), F32))

    source_row = lax.broadcasted_iota(jnp.int32, (2 * columns, LANES), 0)
    lane = lax.broadcasted_iota(jnp.int32, (2 * columns, LANES), 1)
    column = lax.broadcasted_iota(jnp.int32, (2 * columns, count), 0)
    chosen_one = jnp.where(column == picked_ref[...], 1.0, 0.0).astype(BF16)
    place = lax.broadcasted_iota(jnp.int32, (count, LANES), 1) - columns
    place = jnp.where(
        place == lax.broadcasted_iota(jnp.int32, (count, LANES), 0), 1.0, 0.0).astype(BF16)
    select = jnp.dot(chosen_one, place, preferred_element_type=F32)
    select = jnp.where(
        jnp.logical_and(lane < columns, source_row == lane + columns), 1.0, select).astype(BF16)
    high, rest = gram.astype(BF16), gram
    augmented = jnp.dot(high, select, preferred_element_type=F32)
    for _ in range(2):
        rest = rest - high.astype(F32)
        high = rest.astype(BF16)
        augmented = augmented + jnp.dot(high, select, preferred_element_type=F32)
    part1[...] = augmented

    pl.semaphore_wait(barrier, slabs + pencils - 2)
    all_sum(part1, slots1, gathered1, total1, sum_sems[0:6], slabs, pencils)

    tiles = [total1[extra + 8 * t:extra + 8 * (t + 1), :] for t in range(columns // 8)]
    tiles = solve_spd(tiles, columns)
    turned[...] = jnp.zeros_like(turned)
    for t, tile in enumerate(tiles):
        turned[8 * t:8 * (t + 1), :] = tile
    weights[...] = paired(
        turned[...].T[columns:columns + count, 0:columns + extra]).astype(BF16)

    def recycle_layer(z):
        for g in range(groups):
            results = pair_product(
                weights[...], lambda i: rows_of_basis[z, g * GROUP + i], 0, width)
            for i in range(GROUP):
                rec[z + 1, 1 + g * GROUP + i] = results[i]

    def z_copy(side, peer):
        return pltpu.make_async_remote_copy(
            src_ref=z_send.at[side], dst_ref=z_halo.at[side],
            send_sem=halo_send.at[side], recv_sem=halo_recv.at[side],
            device_id={"slab": peer, "pencil": pencil}, device_id_type=MESH)

    def y_copy(side, peer):
        return pltpu.make_async_remote_copy(
            src_ref=y_send.at[side], dst_ref=y_halo.at[side],
            send_sem=halo_send.at[2 + side], recv_sem=halo_recv.at[2 + side],
            device_id={"slab": slab, "pencil": peer}, device_id_type=MESH)

    z_copies = (z_copy(0, lax.rem(slab + 1, slabs)), z_copy(1, lax.rem(slab + slabs - 1, slabs)))
    y_copies = (y_copy(0, lax.rem(pencil + 1, pencils)),
                y_copy(1, lax.rem(pencil + pencils - 1, pencils)))
    sends = (slab < slabs - 1, slab > 0, pencil < pencils - 1, pencil > 0)
    takes = (slab > 0, slab < slabs - 1, pencil > 0, pencil < pencils - 1)

    for side, y in enumerate((height - 1, 0)):
        for first in range(0, depth, GROUP):
            edge = pair_product(weights[...], lambda i: rows_of_basis[first + i, y], 0, width)
            for i in range(GROUP):
                y_send[side, first + i] = edge[i].astype(BF16)
        pl.when(sends[2 + side])(y_copies[side].start)
    recycle_layer(depth - 1)
    z_send[0] = rec[depth, 1:height + 1].astype(BF16)
    pl.when(sends[0])(z_copies[0].start)
    recycle_layer(0)
    z_send[1] = rec[1, 1:height + 1].astype(BF16)
    pl.when(sends[1])(z_copies[1].start)
    pl.loop(1, depth - 1)(recycle_layer)

    lanes = lax.broadcasted_iota(jnp.int32, (count, width), 1)

    def applied_layer(z, normal):
        for g in range(groups):
            values = []
            for y in range(g * GROUP, (g + 1) * GROUP):
                center = rec[z + 1, y + 1]
                beside = rec[z, y + 1] + rec[z + 2, y + 1] + rec[z + 1, y] + rec[z + 1, y + 2]
                beside = beside + jnp.where(lanes == 0, 0.0, pltpu.roll(center, 1, 1))
                beside = beside + jnp.where(
                    lanes == width - 1, 0.0, pltpu.roll(center, width - 1, 1))
                value = factor[z, y:y + 1, :] * center - beside
                values.append(value)
            high, rest = split(jnp.concatenate(values, axis=1))
            both = jnp.concatenate([high, rest], axis=0)
            for i in range(GROUP):
                app_halves[z, g * GROUP + i] = both[:, i * width:(i + 1) * width]
            normal = normal + dot_nt(both, both)
        return normal

    def halve_layer(z):
        for y in range(height):
            high, rest = split(rec[z + 1, y + 1])
            rec_halves[z, y] = jnp.concatenate([high, rest], axis=0)

    pl.loop(0, depth)(halve_layer)
    rec_store = pltpu.make_async_copy(rec_halves, rec_out, out_sems.at[0])
    rec_store.start()
    for side, take in enumerate(takes[2:]):
        pl.when(take)(y_copies[side].wait_recv)

        @pl.when(jnp.logical_not(take))
        def _():
            y_halo[side] = jnp.zeros(y_halo.shape[1:], BF16)

        rec[1:depth + 1, 0 if side == 0 else height + 1] = y_halo[side].astype(F32)
    normal = lax.fori_loop(1, depth - 1, applied_layer, jnp.zeros((2 * count, 2 * count), F32))
    for side, take in enumerate(takes[:2]):
        pl.when(take)(z_copies[side].wait_recv)

        @pl.when(jnp.logical_not(take))
        def _():
            z_halo[side] = jnp.zeros(z_halo.shape[1:], BF16)

        rec[0 if side == 0 else depth + 1, 1:height + 1] = z_halo[side].astype(F32)
        normal = applied_layer(0 if side == 0 else depth - 1, normal)
    app_store = pltpu.make_async_copy(app_halves, app_out, out_sems.at[1])
    app_store.start()

    turned[0:2 * count, 0:2 * count] = normal
    halves = turned[0:count, :] + turned[count:2 * count, :]
    halves = halves + pltpu.roll(halves, LANES - count, 1)
    lane = lax.broadcasted_iota(jnp.int32, (8, LANES), 1)
    packed = halves[0:8]
    for t in range(1, count // 8):
        packed = jnp.where(
            lane < t * count, packed, pltpu.roll(halves[8 * t:8 * (t + 1)], t * count, 1))
    packed, pencil_copies = gather_sum(
        packed, slots2, sum_sems[6], sum_sems[7], "pencil", pencils)
    packed, slab_copies = gather_sum(
        packed, gathered2, sum_sems[8], sum_sems[9], "slab", slabs)
    total2 = jnp.concatenate(
        [packed] + [pltpu.roll(packed, LANES - t * count, 1) for t in range(1, count // 8)], axis=0)

    row = lax.broadcasted_iota(jnp.int32, (count, LANES), 0)
    lane = lax.broadcasted_iota(jnp.int32, (count, LANES), 1)
    matrix = jnp.where(
        lane < count, total2 * (1.0 / cells), jnp.where(lane == row + count, 1.0, 0.0))
    tiles = eliminate([matrix[8 * t:8 * (t + 1), :] for t in range(count // 8)], count)
    inverse = pltpu.roll(jnp.concatenate(tiles, axis=0), LANES - count, 1)
    inverse = jnp.where(lane <= row, inverse, 0.0)
    high = inverse.astype(BF16).astype(F32)
    rest = (inverse - high).astype(BF16).astype(F32)
    inverse_out[...] = high + pltpu.roll(high, count, 1) + pltpu.roll(rest, 2 * count, 1)

    for copy in pencil_copies + slab_copies:
        copy.wait_send()
    for copy, send in zip(z_copies + y_copies, sends):
        pl.when(send)(copy.wait_send)
    rec_store.wait()
    app_store.wait()


def final_kernel(
    inverse_ref, rec_ref, app_ref, rec_out, app_out,
    rec_in, app_in, rec_turned, app_turned, rec_wide, app_wide, in_sems, out_sems,
):
    depth, height, both, width = rec_in.shape
    count = both // 2
    pitch = height + PITCH_EXTRA
    arrays = ((rec_ref, rec_in, rec_wide, rec_turned, rec_out),
              (app_ref, app_in, app_wide, app_turned, app_out))

    def load(z, which):
        return pltpu.make_async_copy(
            arrays[which][0].at[z], arrays[which][1].at[z], in_sems.at[2 * z + which])

    def store(z, which):
        return pltpu.make_async_copy(
            arrays[which][3].at[z], arrays[which][4].at[:, z], out_sems.at[2 * z + which])

    for z in range(depth):
        for which in range(2):
            load(z, which).start()
    factors = paired(inverse_ref[...][:, 0:3 * count]).astype(BF16)

    @pl.loop(0, depth)
    def _(z):
        for which, (_, source, wide, turned, _) in enumerate(arrays):
            load(z, which).wait()
            for g in range(height // GROUP):
                results = pair_product(factors, lambda i: source[z, g * GROUP + i], count, width)
                for i in range(GROUP):
                    wide[pl.ds(g * GROUP + i, count, stride=pitch), :] = results[i]
            for k in range(count):
                turned[z, k] = wide[pl.ds(k * pitch, height), :]
            store(z, which).start()

    for z in range(depth):
        for which in range(2):
            store(z, which).wait()


def local(slabs, pencils, basis, image, material, picked):
    columns, depth, height, width = basis.shape
    count = picked.shape[0]
    extra = 16 - columns % 16 if columns % 16 else 0
    padded = columns + extra
    cells = depth * height * width * slabs * pencils

    def sum_scratch(rows):
        return [
            pltpu.VMEM((rows, LANES), F32),
            pltpu.VMEM((pencils - 1, rows // pencils, LANES), F32),
            pltpu.VMEM((slabs, rows // pencils, LANES), F32),
            pltpu.VMEM((rows, LANES), F32),
        ]

    def sum_sems(*counts):
        return [pltpu.SemaphoreType.DMA((n - 1,)) for n in counts]

    in_vmem = pl.BlockSpec(memory_space=pltpu.VMEM)
    anywhere = pl.BlockSpec(memory_space=pl.ANY)
    turned_shape = jax.ShapeDtypeStruct((depth, height, 2 * count, width), BF16)
    rec, app, inverse = pl.pallas_call(
        functools.partial(main_kernel, slabs, pencils, count, cells),
        out_shape=(turned_shape, turned_shape, jax.ShapeDtypeStruct((count, LANES), F32)),
        in_specs=[anywhere, anywhere, in_vmem, in_vmem],
        out_specs=(anywhere, anywhere, in_vmem),
        scratch_shapes=[
            pltpu.VMEM((depth, columns, height, width), BF16),
            pltpu.VMEM((depth, columns, height, width), BF16),
            pltpu.VMEM((2 * columns * (height + PITCH_EXTRA), width), F32),
            pltpu.VMEM((depth, height, padded, width), BF16),
            pltpu.VMEM((2 * count, 2 * padded), BF16),
            pltpu.VMEM((depth + 2, height + 2, count, width), F32),
            pltpu.VMEM((depth, height, 2 * count, width), BF16),
            pltpu.VMEM((depth, height, 2 * count, width), BF16),
            pltpu.VMEM((depth, height, width), F32),
            pltpu.VMEM((2, height, count, width), BF16),
            pltpu.VMEM((2, height, count, width), BF16),
            pltpu.VMEM((2, depth, count, width), BF16),
            pltpu.VMEM((2, depth, count, width), BF16),
            *sum_scratch(padded),
            pltpu.VMEM((pencils, 8, LANES), F32),
            pltpu.VMEM((slabs, 8, LANES), F32),
            pltpu.VMEM((LANES, LANES), F32),
            pltpu.SemaphoreType.DMA((2 * depth,)),
            pltpu.SemaphoreType.DMA((2,)),
            pltpu.SemaphoreType.DMA((4,)),
            pltpu.SemaphoreType.DMA((4,)),
            *sum_sems(pencils, pencils, slabs, slabs, pencils, pencils),
            *sum_sems(pencils, pencils, slabs, slabs),
        ],
        compiler_params=pltpu.CompilerParams(
            collective_id=0, has_side_effects=True, vmem_limit_bytes=56 * 1024 * 1024),
        name="recycle_update",
    )(basis, image, material, picked[None, :])
    out = jax.ShapeDtypeStruct((count, depth, height, width), F32)
    return pl.pallas_call(
        final_kernel,
        out_shape=(out, out),
        in_specs=[in_vmem, anywhere, anywhere],
        out_specs=(anywhere, anywhere),
        scratch_shapes=[
            *[pltpu.VMEM((depth, height, 2 * count, width), BF16)] * 2,
            *[pltpu.VMEM((depth, count, height, width), F32)] * 2,
            *[pltpu.VMEM((count * (height + PITCH_EXTRA), width), F32)] * 2,
            pltpu.SemaphoreType.DMA((2 * depth,)),
            pltpu.SemaphoreType.DMA((2 * depth,)),
        ],
        compiler_params=pltpu.CompilerParams(vmem_limit_bytes=60 * 1024 * 1024),
        name="times_inverse",
    )(inverse, rec, app)


def solution(mesh):
    placed = (
        P(None, "slab", "pencil", None),
        P(None, "slab", "pencil", None),
        P("slab", "pencil", None),
        P(),
    )
    return jax.shard_map(
        functools.partial(local, mesh.shape["slab"], mesh.shape["pencil"]),
        mesh=mesh,
        in_specs=placed,
        out_specs=(P(None, "slab", "pencil", None), P(None, "slab", "pencil", None)),
        check_vma=False,
    )
```
